256 devices in a mesh: smp: 8 (over x, core), ctx: 32 (over y, z).
Axes of the slice: x: 4, y: 4, z: 8, core: 2. Of those that a mesh axis runs over, the one named last changes fastest.
Arguments:
- query: bfloat16 [8, 4096, 4096], P('smp', 'ctx'), may hold values from -6 to 6
- d_out: bfloat16 [8, 4096, 4096], P('smp', 'ctx'), may hold values from -6 to 6
- branch_kv: bfloat16 [8, 4096, 1024], P('smp', 'ctx'), may hold values from -6 to 6
- prefix_kv: bfloat16 [1024, 1024], P('ctx', 'smp'), may hold values from -6 to 6
- parents: int32 [8, 32], P('smp'), may hold values from -1 to 30, as said below
- lengths: int32 [8, 32], P('smp'), may hold values from 33 to 128, as said below
Outputs:
- attn_out: bfloat16 [8, 4096, 4096], P('smp', 'ctx')
- d_query: bfloat16 [8, 4096, 4096], P('smp', 'ctx')
- d_branch_kv: bfloat16 [8, 4096, 1024], P('smp', 'ctx')
- d_prefix_kv: bfloat16 [1024, 1024], P('ctx', 'smp')
The draws below stay inside these ranges and needn't reach their ends.
Inputs may be any that keep to these rules, and one draw needn't show every extreme that they name: parents[s, 0] = -1; for i > 0 parents[s, i] lies below i; every path from the prefix to a block has at most 8 blocks, the block included, and block 7 of every sample has exactly 8; parents[s, 31] = 30. lengths[s, 0] = 128 and lengths[s, 1] = 33.
All inputs are finite; a program needn't handle non-finite values.
Results may differ from the reference program's by a relative error of at most 0.03.
Values may be sent and summed in bfloat16 or wider, within the bound.
No kernel may reach another device: no remote copies, remote signals or barrier semaphores. Data moves between devices by JAX's collectives and lax.ppermute only.
A program may use at most 128 MiB of HBM per device.

```python
import jax
import jax.numpy as jnp
from jax import lax

HQ = 32
HK = 4
HD = 128
FEAT = 1024
BLOCK = 128
PREFIX = 1024
NB = 32
BTOK = 4096
DEPTH = 8
SAMPLES = 8


def draw_prefix_kv(key, part):
    key = jax.random.fold_in(key, 11)
    base_draw = jnp.clip(jax.random.normal(key, (PREFIX, FEAT), jnp.float32), -6.0, 6.0)
    return base_draw.astype(jnp.bfloat16)


def draw_query(key, part):
    key = jax.random.fold_in(key, 13)
    base_draw = jnp.clip(jax.random.normal(key, (SAMPLES, BTOK, HQ * HD), jnp.float32), -6.0, 6.0)
    return base_draw.astype(jnp.bfloat16)


def draw_parents(key, part):
    key = jax.random.fold_in(key, 5)
    coin_key, target_key = jax.random.split(key)
    coins = jax.random.randint(coin_key, (SAMPLES, NB), 0, 2, dtype=jnp.int32)
    jump_target = jax.random.randint(target_key, (SAMPLES, NB), 0, DEPTH - 1, dtype=jnp.int32)
    path_limit = DEPTH

    def one_sample(inputs):
        coin_row, jump_row = inputs

        def scan_step(path_depth, step_inputs):
            index, coin, target = step_inputs
            chain = index < path_limit
            force_jump = index == NB - 2
            force_grow = index == NB - 1
            target = jnp.where(force_jump, jnp.minimum(target, path_limit - 3), target)
            grows = chain | force_grow | jnp.logical_not(force_jump) & (path_depth < path_limit) & (coin == 1)
            parent = jnp.where(index == 0, -1, jnp.where(grows, index - 1, target))
            new_depth = jnp.where(index == 0, 1, jnp.where(grows, path_depth + 1, target + 2))
            return (new_depth.astype(jnp.int32), parent.astype(jnp.int32))
        _, parent_row = lax.scan(scan_step, jnp.int32(0), (jnp.arange(NB, dtype=jnp.int32), coin_row, jump_row))
        return parent_row
    return jax.vmap(one_sample)((coins, jump_target))


def draw_lengths(key, part):
    key = jax.random.fold_in(key, 7)
    drawn = BLOCK // 4 + 1 + jax.random.randint(key, (SAMPLES, NB), 0, BLOCK - BLOCK // 4, dtype=jnp.int32)
    drawn = drawn.at[:, 0].set(BLOCK)
    drawn = drawn.at[:, 1].set(BLOCK // 4 + 1)
    return drawn


def levels(rng, shape, cuts, low, top_value):
    def one(dim, parts):
        draws = jax.random.uniform(jax.random.fold_in(jax.random.fold_in(rng, 6), dim), (parts,), jnp.float32, low / len(cuts), top_value / len(cuts))
        return jnp.repeat(jnp.exp(draws), shape[dim] // parts).reshape((-1,) + (1,) * (len(shape) - dim - 1))

    factor_of = one(*cuts[0])
    for cut in cuts[1:]:
        factor_of = factor_of * one(*cut)
    return factor_of


def centred(rng, dims, spread, limit, cuts=(), held_as=jnp.bfloat16):
    level = levels(rng, dims, cuts, -0.22, 0.18) if cuts else 1.0
    values = jax.random.normal(rng, dims, jnp.float32) * spread * level
    return jnp.minimum(jnp.maximum(values, -limit), limit).astype(held_as)


def setup_inputs(seed: int = 0) -> dict:
    seeds = jax.random.split(jax.random.key(seed), 7)
    query = draw_query(jax.random.fold_in(seeds[6], 71), 0)
    d_out = centred(seeds[1], (SAMPLES, BTOK, HQ * HD), 1.0, 6.0, ((0, 8), (1, 32)))
    branch_kv = centred(seeds[2], (SAMPLES, BTOK, FEAT), 1.0, 6.0, ((0, 8), (1, 32)))
    prefix_kv = draw_prefix_kv(jax.random.fold_in(seeds[6], 71), 0)
    parents = draw_parents(jax.random.fold_in(seeds[6], 71), 0)
    lengths = draw_lengths(jax.random.fold_in(seeds[6], 71), 0)
    return {"query": query, "d_out": d_out, "branch_kv": branch_kv, "prefix_kv": prefix_kv, "parents": parents, "lengths": lengths}


def build_masks(parent_row, length_row, block_index, depth_slots, block_rows, prefix_rows):
    num_blocks = parent_row.shape[0]
    indices = jnp.arange(num_blocks, dtype=jnp.int32)
    parent_links = (parent_row[:, None] == indices[None, :]).astype(jnp.float32)
    reachable = jnp.eye(num_blocks, dtype=jnp.float32) + parent_links
    for _ in range(num_blocks.bit_length()):
        reachable = jnp.minimum(jnp.dot(reachable, reachable, precision=lax.Precision.HIGHEST), 1.0)
    pick_row = (indices == block_index).astype(jnp.float32)
    ancestry = jnp.dot(pick_row, reachable, precision=lax.Precision.HIGHEST)
    position = jnp.cumsum(ancestry) - 1.0
    slot_ids = jnp.arange(depth_slots, dtype=jnp.float32)
    selector = ancestry[None, :] * (position[None, :] == slot_ids[:, None]).astype(jnp.float32)
    block_float = indices.astype(jnp.float32)
    owner_block = jnp.dot(selector, block_float, precision=lax.Precision.HIGHEST)
    slot_used = jnp.sum(selector, axis=1) > 0.5
    own_slot = slot_used & (jnp.abs(owner_block - jnp.sum(pick_row * block_float)) < 0.5)
    lengths_float = length_row.astype(jnp.float32)
    slot_length = jnp.dot(selector, lengths_float, precision=lax.Precision.HIGHEST)
    own_length = jnp.sum(pick_row * lengths_float)
    place = jnp.arange(block_rows, dtype=jnp.float32)
    row_place = place[:, None, None]
    key_place = place[None, None, :]
    slot_allowed = slot_used[None, :, None] & (key_place < slot_length[None, :, None]) & (
        jnp.logical_not(own_slot)[None, :, None] | (key_place <= row_place))
    key_allowed = jnp.concatenate(
        [jnp.ones((block_rows, prefix_rows), dtype=jnp.bool_),
         slot_allowed.reshape(block_rows, depth_slots * block_rows)], axis=1)
    row_valid = place < own_length
    return selector, key_allowed, row_valid


def attend(query_block, dout_block, key_values, key_allowed, row_valid, heads_kv, head_dim):
    row_count = query_block.shape[0]
    query_width = query_block.shape[1]
    group_size = query_width // (heads_kv * head_dim)
    key_count = key_values.shape[0]
    softmax_scale = head_dim ** -0.5
    grad_live = jnp.where(row_valid[:, None], dout_block, jnp.zeros_like(dout_block))
    query_heads = query_block.reshape(row_count, heads_kv, group_size, head_dim).transpose(1, 0, 2, 3).reshape(
        heads_kv, row_count * group_size, head_dim)
    grad_heads = grad_live.reshape(row_count, heads_kv, group_size, head_dim).transpose(1, 0, 2, 3).reshape(
        heads_kv, row_count * group_size, head_dim)
    key_heads = key_values[:, : heads_kv * head_dim].reshape(key_count, heads_kv, head_dim).transpose(1, 0, 2)
    value_heads = key_values[:, heads_kv * head_dim:].reshape(key_count, heads_kv, head_dim).transpose(1, 0, 2)
    mask_rows = jnp.repeat(key_allowed, group_size, axis=0)
    live_rows = jnp.repeat(row_valid, group_size)

    def one_head(inputs):
        query_head, grad_head, key_head, value_head = inputs
        scores = jnp.dot(query_head, key_head.T, preferred_element_type=jnp.float32) * softmax_scale
        scores = jnp.where(mask_rows, scores, -jnp.inf)
        row_max = jnp.max(scores, axis=1, keepdims=True)
        exponent = jnp.exp(scores - row_max)
        probability = exponent / jnp.sum(exponent, axis=1, keepdims=True)
        prob_round = probability.astype(jnp.bfloat16)
        attended = jnp.dot(prob_round, value_head, preferred_element_type=jnp.float32)
        attended_out = jnp.where(live_rows[:, None], attended, 0.0).astype(jnp.bfloat16)
        grad_probs = jnp.dot(grad_head, value_head.T, preferred_element_type=jnp.float32)
        row_delta = jnp.sum(grad_head.astype(jnp.float32) * attended_out.astype(jnp.float32), axis=1, keepdims=True)
        grad_scores = (probability * (grad_probs - row_delta)).astype(jnp.bfloat16)
        grad_query = (jnp.dot(grad_scores, key_head, preferred_element_type=jnp.float32) * softmax_scale).astype(jnp.bfloat16)
        grad_keys = jnp.dot(grad_scores.T, query_head, preferred_element_type=jnp.float32) * softmax_scale
        grad_values = jnp.dot(prob_round.T, grad_head, preferred_element_type=jnp.float32)
        return attended_out, grad_query, grad_keys, grad_values

    attended_all, grad_query_all, grad_keys_all, grad_values_all = lax.map(
        one_head, (query_heads, grad_heads, key_heads, value_heads))
    output = attended_all.reshape(heads_kv, row_count, group_size, head_dim).transpose(1, 0, 2, 3).reshape(row_count, query_width)
    grad_query_out = grad_query_all.reshape(heads_kv, row_count, group_size, head_dim).transpose(1, 0, 2, 3).reshape(row_count, query_width)
    grad_pairs = jnp.concatenate(
        [grad_keys_all.transpose(1, 0, 2).reshape(key_count, heads_kv * head_dim),
         grad_values_all.transpose(1, 0, 2).reshape(key_count, heads_kv * head_dim)], axis=1)
    return output, grad_query_out, grad_pairs


def reference(query, d_out, branch_kv, prefix_kv, parents, lengths):
    def one_sample(inputs):
        query_sample, dout_sample, pairs_sample, parent_row, length_row = inputs
        blocks_kv = pairs_sample.reshape(NB, BLOCK, FEAT)

        def scan_step(totals, block_index):
            grad_blocks, grad_prefix = totals
            start_row = (block_index * BLOCK).astype(jnp.int32)
            query_block = lax.dynamic_slice_in_dim(query_sample, start_row, BLOCK, 0)
            dout_block = lax.dynamic_slice_in_dim(dout_sample, start_row, BLOCK, 0)
            selector, key_allowed, row_valid = build_masks(parent_row, length_row, block_index, DEPTH, BLOCK, PREFIX)
            picked = jnp.einsum("kn,nbf->kbf", selector, blocks_kv.astype(jnp.float32),
                                precision=lax.Precision.HIGHEST).astype(jnp.bfloat16)
            key_values = jnp.concatenate([prefix_kv, picked.reshape(DEPTH * BLOCK, FEAT)], axis=0)
            output, grad_query, grad_pairs = attend(query_block, dout_block, key_values, key_allowed, row_valid, HK, HD)
            grad_prefix = grad_prefix + grad_pairs[:PREFIX]
            slot_grads = grad_pairs[PREFIX:].reshape(DEPTH, BLOCK, FEAT)
            grad_blocks = grad_blocks + jnp.einsum("kn,kbf->nbf", selector, slot_grads, precision=lax.Precision.HIGHEST)
            return (grad_blocks, grad_prefix), (output, grad_query)

        initial = (jnp.zeros((NB, BLOCK, FEAT), jnp.float32), jnp.zeros((PREFIX, FEAT), jnp.float32))
        (grad_blocks, grad_prefix), (outputs, grad_queries) = lax.scan(
            scan_step, initial, jnp.arange(NB, dtype=jnp.int32))
        return (outputs.reshape(BTOK, HQ * HD), grad_queries.reshape(BTOK, HQ * HD),
                grad_blocks.reshape(BTOK, FEAT), grad_prefix)

    outputs, grad_queries, grad_branch, grad_prefix = lax.map(
        one_sample, (query, d_out, branch_kv, parents, lengths))
    return outputs, grad_queries, grad_branch.astype(jnp.bfloat16), jnp.sum(grad_prefix, axis=0).astype(jnp.bfloat16)
```

```python
import functools

import jax
import jax.numpy as jnp
from jax import lax
from jax.experimental import pallas as pl
from jax.experimental.pallas import tpu as pltpu
from jax.sharding import Mesh, PartitionSpec as P

HK = 4
HD = 128
GROUP = 8
BLOCK = 128
NB = 32
DEPTH = 8
PREFIX = 1024
ROWS = GROUP * BLOCK
CHUNK = 256
SCALE = HD ** -0.5
SCALE_LOG2E = SCALE * 1.4426950408889634
MASKED = -1e30
F32 = jnp.float32
BF16 = jnp.bfloat16


def dot(a, b):
    return lax.dot_general(a, b, (((1,), (0,)), ((), ())), preferred_element_type=F32)


def dot_t(a, b):
    return lax.dot_general(a, b, (((1,), (1,)), ((), ())), preferred_element_type=F32)


def attend_kernel(
    parents, lengths, block_ids, place,
    q_ref, g_ref, bk_ref, bv_ref, pk_ref, pv_ref,
    o_ref, dq_ref, dbk_ref, dbv_ref, dpk_ref, dpv_ref,
    qt, gt, qlt, glt, pkt, pvt, sk, sv, skt, svt, scores, probs, acc, bias,
    abk, abv, apk, apv,
):
    step = pl.program_id(0)
    block = block_ids[step]
    live = lengths[block]

    @pl.when(step == 0)
    def _():
        pkt[...] = pk_ref[...].T
        pvt[...] = pv_ref[...].T
        abk[...] = jnp.zeros_like(abk)
        abv[...] = jnp.zeros_like(abv)
        apk[...] = jnp.zeros_like(apk)
        apv[...] = jnp.zeros_like(apv)

    row_live = lax.broadcasted_iota(jnp.int32, (HD, BLOCK), 1) < live
    for h in range(GROUP):
        cols = slice(h * BLOCK, (h + 1) * BLOCK)
        qt[:, cols] = q_ref[0, :, cols].T
        gt[:, cols] = jnp.where(row_live, g_ref[0, :, cols].astype(F32).T, 0.0).astype(BF16)

    slots, used = [], []
    current = block
    for k in range(DEPTH):
        in_use = current >= 0
        slot = jnp.where(in_use, current, block)
        slots.append(slot)
        used.append(in_use)
        current = jnp.where(in_use, parents[slot], -1)
    key_row = lax.broadcasted_iota(jnp.int32, (BLOCK, BLOCK), 0)
    query_row = lax.broadcasted_iota(jnp.int32, (BLOCK, BLOCK), 1)
    for k in range(DEPTH):
        rows = slice(k * BLOCK, (k + 1) * BLOCK)

        @pl.when(used[k & ~1])
        def _(k=k, rows=rows):
            at = place[slots[k]]
            key = bk_ref[at]
            value = bv_ref[at]
            sk[rows, :] = key
            sv[rows, :] = value
            skt[:, rows] = key.T
            svt[:, rows] = value.T
            seen = key_row < jnp.where(used[k], lengths[slots[k]], 0)
            if k == 0:
                seen = seen & (key_row <= query_row)
            bias[rows, :] = jnp.where(seen, 0.0, MASKED)

    pairs = DEPTH // 2
    top = jnp.full((8, ROWS), MASKED, F32)
    for c in range(PREFIX // CHUNK):
        keys = slice(c * CHUNK, (c + 1) * CHUNK)
        s = dot(pk_ref[keys, :], qt[...])
        scores[keys, :] = s
        top = jnp.maximum(top, jnp.max(s.reshape(CHUNK // 8, 8, ROWS), axis=0))
    acc[0:8, :] = top
    for j in range(pairs):
        @pl.when(used[2 * j])
        def _(j=j):
            rows = slice(j * CHUNK, (j + 1) * CHUNK)
            s = dot(sk[rows, :], qt[...])
            s = s + jnp.concatenate([bias[rows, :]] * GROUP, axis=1)
            scores[PREFIX + j * CHUNK:PREFIX + (j + 1) * CHUNK, :] = s
            acc[0:8, :] = jnp.maximum(acc[0:8, :], jnp.max(s.reshape(CHUNK // 8, 8, ROWS), axis=0))
    peak = jnp.max(acc[0:8, :], axis=0, keepdims=True) * SCALE_LOG2E

    total = jnp.zeros((8, ROWS), F32)
    out_t = jnp.zeros((HD, ROWS), F32)
    for c in range(PREFIX // CHUNK):
        keys = slice(c * CHUNK, (c + 1) * CHUNK)
        e = jnp.exp2(scores[keys, :] * SCALE_LOG2E - peak)
        total = total + jnp.sum(e.reshape(CHUNK // 8, 8, ROWS), axis=0)
        low = e.astype(BF16)
        probs[keys, :] = low
        out_t = out_t + dot(pvt[:, keys], low)
    acc[0:HD, :] = out_t
    acc[HD:HD + 8, :] = total
    for j in range(pairs):
        @pl.when(used[2 * j])
        def _(j=j):
            rows = slice(j * CHUNK, (j + 1) * CHUNK)
            keys = slice(PREFIX + j * CHUNK, PREFIX + (j + 1) * CHUNK)
            e = jnp.exp2(scores[keys, :] * SCALE_LOG2E - peak)
            acc[HD:HD + 8, :] += jnp.sum(e.reshape(CHUNK // 8, 8, ROWS), axis=0)
            low = e.astype(BF16)
            probs[keys, :] = low
            acc[0:HD, :] += dot(svt[:, rows], low)
    inverse = 1.0 / jnp.sum(acc[HD:HD + 8, :], axis=0, keepdims=True)

    out_t = acc[0:HD, :] * inverse
    grad_t = gt[...].astype(F32)
    delta = jnp.sum(grad_t * out_t.astype(BF16).astype(F32), axis=0, keepdims=True)
    glt[...] = (grad_t * inverse).astype(BF16)
    qlt[...] = (qt[...].astype(F32) * (inverse * SCALE)).astype(BF16)
    for h in range(GROUP):
        cols = slice(h * BLOCK, (h + 1) * BLOCK)
        o_ref[0, :, cols] = jnp.where(row_live, out_t[:, cols], 0.0).T.astype(BF16)

    dq_t = jnp.zeros((HD, ROWS), F32)
    for c in range(PREFIX // CHUNK):
        keys = slice(c * CHUNK, (c + 1) * CHUNK)
        low = probs[keys, :]
        ds = (low.astype(F32) * (dot(pv_ref[keys, :], gt[...]) - delta)).astype(BF16)
        apv[keys, :] += dot_t(low, glt[...])
        apk[keys, :] += dot_t(ds, qlt[...])
        dq_t = dq_t + dot(pkt[:, keys], ds)
    acc[0:HD, :] = dq_t
    for j in range(pairs):
        @pl.when(used[2 * j])
        def _(j=j):
            rows = slice(j * CHUNK, (j + 1) * CHUNK)
            keys = slice(PREFIX + j * CHUNK, PREFIX + (j + 1) * CHUNK)
            low = probs[keys, :]
            ds = (low.astype(F32) * (dot(sv[rows, :], gt[...]) - delta)).astype(BF16)
            dv = dot_t(low, glt[...])
            dk = dot_t(ds, qlt[...])
            for k in range(2):
                at = place[slots[2 * j + k]]
                abv[at] += dv[k * BLOCK:(k + 1) * BLOCK]
                abk[at] += dk[k * BLOCK:(k + 1) * BLOCK]
            acc[0:HD, :] += dot(skt[:, rows], ds)
    dq_t = acc[0:HD, :] * (inverse * SCALE)
    for h in range(GROUP):
        cols = slice(h * BLOCK, (h + 1) * BLOCK)
        dq_ref[0, :, cols] = dq_t[:, cols].T.astype(BF16)

    @pl.when(step == pl.num_programs(0) - 1)
    def _():
        dbk_ref[...] = abk[...].astype(BF16)
        dbv_ref[...] = abv[...].astype(BF16)
        dpk_ref[...] = apk[...].astype(BF16)
        dpv_ref[...] = apv[...].astype(BF16)


def attend(parents, lengths, block_ids, place, q, g, bk, bv, pk, pv):
    whole = lambda shape: pl.BlockSpec(shape, lambda i, *_: (0,) * len(shape))
    heads = pl.BlockSpec((1, BLOCK, ROWS), lambda i, *_: (i, 0, 0))
    blocks, prefix = (NB, BLOCK, HD), (PREFIX, HD)
    struct = jax.ShapeDtypeStruct
    wide = lambda rows, dtype: pltpu.VMEM((rows, ROWS), dtype)
    return pl.pallas_call(
        attend_kernel,
        grid_spec=pltpu.PrefetchScalarGridSpec(
            num_scalar_prefetch=4,
            grid=(q.shape[0],),
            in_specs=[heads, heads, whole(blocks), whole(blocks), whole(prefix), whole(prefix)],
            out_specs=[heads, heads, whole(blocks), whole(blocks), whole(prefix), whole(prefix)],
            scratch_shapes=[
                wide(HD, BF16), wide(HD, BF16), wide(HD, BF16), wide(HD, BF16),
                pltpu.VMEM((HD, PREFIX), BF16), pltpu.VMEM((HD, PREFIX), BF16),
                pltpu.VMEM((DEPTH * BLOCK, HD), BF16), pltpu.VMEM((DEPTH * BLOCK, HD), BF16),
                pltpu.VMEM((HD, DEPTH * BLOCK), BF16), pltpu.VMEM((HD, DEPTH * BLOCK), BF16),
                wide(PREFIX + DEPTH * BLOCK, F32), wide(PREFIX + DEPTH * BLOCK, BF16),
                wide(HD + 8, F32), pltpu.VMEM((DEPTH * BLOCK, BLOCK), F32),
                pltpu.VMEM(blocks, F32), pltpu.VMEM(blocks, F32),
                pltpu.VMEM(prefix, F32), pltpu.VMEM(prefix, F32),
            ],
        ),
        out_shape=[
            struct(q.shape, BF16), struct(q.shape, BF16),
            struct(blocks, BF16), struct(blocks, BF16), struct(prefix, BF16), struct(prefix, BF16),
        ],
        compiler_params=pltpu.CompilerParams(vmem_limit_bytes=56 * 1024 * 1024),
        name="attend",
    )(parents, lengths, block_ids, place, q, g, bk, bv, pk, pv)


def per_device(query, d_out, branch_kv, prefix_kv, parents, lengths):
    ny, nz = lax.axis_size("y"), lax.axis_size("z")
    smp = ("x", "core")
    z = lax.axis_index("z")
    exchange = functools.partial(lax.all_to_all, axis_name="y", split_axis=1, concat_axis=0, tiled=True)
    back = functools.partial(lax.all_to_all, axis_name="y", split_axis=0, concat_axis=1, tiled=True)
    half = HK * HD

    prefix_rows = prefix_kv.shape[0]
    with_features = lax.all_gather(prefix_kv, smp, axis=1, tiled=True)
    kv = jnp.concatenate([branch_kv[0], with_features], axis=0)
    k = exchange(kv[:, :half])
    v = exchange(kv[:, half:])
    k = lax.all_gather(k, "z", axis=0, tiled=True).reshape(nz * ny, BLOCK + prefix_rows, HD)
    v = lax.all_gather(v, "z", axis=0, tiled=True).reshape(nz * ny, BLOCK + prefix_rows, HD)
    q = exchange(query[0]).reshape(ny, BLOCK, ROWS)
    g = exchange(d_out[0]).reshape(ny, BLOCK, ROWS)

    block_ids = jnp.arange(ny, dtype=jnp.int32) * nz + z
    ids = jnp.arange(NB, dtype=jnp.int32)
    place = (ids % nz) * ny + ids // nz
    out, dq, dbk, dbv, dpk, dpv = attend(
        parents[0], lengths[0], block_ids, place, q, g,
        k[:, :BLOCK], v[:, :BLOCK],
        k[:, BLOCK:].reshape(PREFIX, HD), v[:, BLOCK:].reshape(PREFIX, HD),
    )

    out = back(out.reshape(ny * BLOCK, ROWS))
    dq = back(dq.reshape(ny * BLOCK, ROWS))
    joined = lambda b, p: jnp.concatenate([b, p.reshape(NB, prefix_rows, HD)], axis=1)
    scatter = functools.partial(lax.psum_scatter, axis_name="z", scatter_dimension=0, tiled=True)
    dk = scatter(joined(dbk, dpk)).reshape(ny * (BLOCK + prefix_rows), HD)
    dv = scatter(joined(dbv, dpv)).reshape(ny * (BLOCK + prefix_rows), HD)
    dkv = jnp.concatenate([back(dk), back(dv)], axis=1)
    terms = lax.all_to_all(dkv[BLOCK:], smp, split_axis=1, concat_axis=0, tiled=True)
    d_prefix = jnp.sum(terms.reshape(-1, prefix_rows, HD).astype(F32), axis=0)
    return out[None], dq[None], dkv[:BLOCK][None], d_prefix.astype(BF16)


def solution(mesh):
    devices = mesh.devices.reshape(4, 2, 4, 8)
    split = Mesh(devices, ("x", "core", "y", "z"))
    smp, ctx = ("x", "core"), ("y", "z")
    return jax.shard_map(
        per_device,
        mesh=split,
        in_specs=(
            P(smp, ctx, None), P(smp, ctx, None), P(smp, ctx, None),
            P(ctx, smp), P(smp, None), P(smp, None),
        ),
        out_specs=(P(smp, ctx, None), P(smp, ctx, None), P(smp, ctx, None), P(ctx, smp)),
        check_vma=False,
    )
```

```python
import jax
import jax.numpy as jnp
from jax import lax
from jax.experimental import pallas as pl
from jax.experimental.pallas import tpu as pltpu
from jax.sharding import Mesh, PartitionSpec as P

HK = 4
HD = 128
GROUP = 8
BLOCK = 128
NB = 32
DEPTH = 8
PREFIX = 1024
ROWS = GROUP * BLOCK
CHUNK = 256
TILE = 64
SCALE = HD ** -0.5
SCALE_LOG2E = SCALE * 1.4426950408889634
MASKED = -1e30
F32 = jnp.float32
BF16 = jnp.bfloat16


def dot(a, b):
    return lax.dot_general(a, b, (((1,), (0,)), ((), ())), preferred_element_type=F32)


def dot_t(a, b):
    return lax.dot_general(a, b, (((1,), (1,)), ((), ())), preferred_element_type=F32)


def my_blocks(step):
    ny, nz = lax.axis_size("y"), lax.axis_size("z")
    return lax.rem(lax.axis_index("y") - step + ny, ny) * nz + lax.axis_index("z")


def place_of(block):
    ny, nz = lax.axis_size("y"), lax.axis_size("z")
    return lax.rem(block, nz) * ny + lax.rem(lax.axis_index("y") - block // nz + ny, ny)


def half_moves(first):
    moves = []
    for feature in range(2 * HK):
        half = first if feature >= HK else 1 - first
        for holder in range(HK):
            moves.append((feature * HK + holder, (holder * 2 + half) * HK + feature % HK))
    return moves


def fold(a):
    return a.reshape(a.shape[0] // 8, 8, a.shape[1])


def head_cols(h):
    return slice(h * BLOCK, (h + 1) * BLOCK)


def prefix_kernel(
    lengths, qg0, qg1, qg2, qg3, prefix,
    qt, gt, probs, out_t, stats, pkt, pvt, scores,
):
    step = pl.program_id(0)

    @pl.when(step == 0)
    def _():
        pkt[...] = prefix[:, :HD].T
        pvt[...] = prefix[:, HD:].T

    row_live = lax.broadcasted_iota(jnp.int32, (HD, BLOCK), 1) < lengths[my_blocks(step)]
    for d, part in enumerate((qg0, qg1, qg2, qg3)):
        @pl.when(step == d)
        def _(part=part):
            for h in range(GROUP):
                cols = head_cols(h)
                qt[0, :, cols] = part[0, :, cols].T
                gt[0, :, cols] = jnp.where(row_live, part[1, :, cols].astype(F32).T, 0.0).astype(BF16)

    top = jnp.full((8, ROWS), MASKED, F32)
    for c in range(PREFIX // CHUNK):
        keys = slice(c * CHUNK, (c + 1) * CHUNK)
        s = dot(prefix[keys, :HD], qt[0])
        scores[keys, :] = s
        top = jnp.maximum(top, jnp.max(fold(s), axis=0))
    top = jnp.max(top, axis=0, keepdims=True)
    peak = top * SCALE_LOG2E
    total = jnp.zeros((8, ROWS), F32)
    acc = jnp.zeros((HD, ROWS), F32)
    for c in range(PREFIX // CHUNK):
        keys = slice(c * CHUNK, (c + 1) * CHUNK)
        e = jnp.exp2(scores[keys, :] * SCALE_LOG2E - peak)
        total = total + jnp.sum(fold(e), axis=0)
        low = e.astype(BF16)
        probs[0, keys, :] = low
        acc = acc + dot(pvt[:, keys], low)
    out_t[0] = acc
    stats[0, 0:1, :] = top
    stats[0, 1:2, :] = jnp.sum(total, axis=0, keepdims=True)


def branch_kernel(
    parents, lengths, qt, gt, prefix_out, stats, kv,
    out, dq_part, glp, qlp, rows_out, dkv,
    qlt, glt, sk, sv, skt, svt, scores, probs, acc, bias, abk, abv,
):
    step = pl.program_id(0)
    block = my_blocks(step)
    live = lengths[block]

    @pl.when(step == 0)
    def _():
        abk[...] = jnp.zeros_like(abk)
        abv[...] = jnp.zeros_like(abv)

    slots, used = [], []
    current = block
    for k in range(DEPTH):
        in_use = current >= 0
        slot = jnp.where(in_use, current, block)
        slots.append(slot)
        used.append(in_use)
        current = jnp.where(in_use, parents[slot], -1)
    key_row = lax.broadcasted_iota(jnp.int32, (BLOCK, BLOCK), 0)
    query_row = lax.broadcasted_iota(jnp.int32, (BLOCK, BLOCK), 1)
    pairs = DEPTH // 2
    acc[0:8, :] = jnp.broadcast_to(stats[0, 0:1, :], (8, ROWS))
    for j in range(pairs):
        @pl.when(used[2 * j])
        def _(j=j):
            for k in (2 * j, 2 * j + 1):
                rows = head_cols(k)
                at = place_of(slots[k])
                key = kv[at, 0]
                value = kv[at, 1]
                sk[rows, :] = key
                sv[rows, :] = value
                skt[:, rows] = key.T
                svt[:, rows] = value.T
                seen = key_row < jnp.where(used[k], lengths[slots[k]], 0)
                if k == 0:
                    seen = seen & (key_row <= query_row)
                bias[rows, :] = jnp.where(seen, 0.0, MASKED)
            rows = slice(j * CHUNK, (j + 1) * CHUNK)
            s = dot(sk[rows, :], qt[0])
            s = s + jnp.concatenate([bias[rows, :]] * GROUP, axis=1)
            scores[rows, :] = s
            acc[0:8, :] = jnp.maximum(acc[0:8, :], jnp.max(fold(s), axis=0))
    peak = jnp.max(acc[0:8, :], axis=0, keepdims=True) * SCALE_LOG2E

    acc[...] = jnp.zeros_like(acc)
    for j in range(pairs):
        @pl.when(used[2 * j])
        def _(j=j):
            rows = slice(j * CHUNK, (j + 1) * CHUNK)
            e = jnp.exp2(scores[rows, :] * SCALE_LOG2E - peak)
            acc[HD:HD + 8, :] += jnp.sum(fold(e), axis=0)
            low = e.astype(BF16)
            probs[rows, :] = low
            acc[0:HD, :] += dot(svt[:, rows], low)

    alpha = jnp.exp2(stats[0, 0:1, :] * SCALE_LOG2E - peak)
    total = alpha * stats[0, 1:2, :] + jnp.sum(acc[HD:HD + 8, :], axis=0, keepdims=True)
    inverse = 1.0 / total
    prefix_inverse = alpha * inverse
    out_t = acc[0:HD, :] * inverse + prefix_out[0] * prefix_inverse
    grad_t = gt[0].astype(F32)
    query_t = qt[0].astype(F32)
    delta = jnp.sum(grad_t * out_t.astype(BF16).astype(F32), axis=0, keepdims=True)
    glt[...] = (grad_t * inverse).astype(BF16)
    qlt[...] = (query_t * (inverse * SCALE)).astype(BF16)
    glp[0] = (grad_t * prefix_inverse).astype(BF16)
    qlp[0] = (query_t * (prefix_inverse * SCALE)).astype(BF16)
    rows_out[0, 0:1, :] = delta
    rows_out[0, 1:2, :] = prefix_inverse * SCALE
    row_live = lax.broadcasted_iota(jnp.int32, (HD, BLOCK), 1) < live
    for h in range(GROUP):
        cols = head_cols(h)
        out[0, :, cols] = jnp.where(row_live, out_t[:, cols], 0.0).T.astype(BF16)

    acc[0:HD, :] = jnp.zeros((HD, ROWS), F32)
    for j in range(pairs):
        @pl.when(used[2 * j])
        def _(j=j):
            rows = slice(j * CHUNK, (j + 1) * CHUNK)
            low = probs[rows, :]
            ds = (low.astype(F32) * (dot(sv[rows, :], gt[0]) - delta)).astype(BF16)
            dv = dot_t(low, glt[...])
            dk = dot_t(ds, qlt[...])
            for k in range(2):
                at = place_of(slots[2 * j + k])
                abv[at] += dv[k * BLOCK:(k + 1) * BLOCK]
                abk[at] += dk[k * BLOCK:(k + 1) * BLOCK]
            acc[0:HD, :] += dot(skt[:, rows], ds)
    dq_part[0] = acc[0:HD, :] * (inverse * SCALE)

    @pl.when(step == pl.num_programs(0) - 1)
    def _():
        dkv[:, 0] = abk[...].astype(BF16)
        dkv[:, 1] = abv[...].astype(BF16)


def prefix_back_kernel(
    gt, probs, glp, qlp, rows_in, dq_part, out, pkt, prefix, both, dp, apk, apv,
):
    step = pl.program_id(0)

    @pl.when(step == 0)
    def _():
        apk[...] = jnp.zeros_like(apk)
        apv[...] = jnp.zeros_like(apv)

    delta = rows_in[0, 0:1, :]
    acc = jnp.zeros((HD, ROWS), F32)
    for c in range(PREFIX // CHUNK):
        keys = slice(c * CHUNK, (c + 1) * CHUNK)
        low = probs[0, keys, :]
        ds = (low.astype(F32) * (dot(prefix[keys, HD:], gt[0]) - delta)).astype(BF16)
        apv[keys, :] += dot_t(low, glp[0])
        apk[keys, :] += dot_t(ds, qlp[0])
        acc = acc + dot(pkt[:, keys], ds)
    dq_t = acc * rows_in[0, 1:2, :] + dq_part[0]
    for h in range(GROUP):
        cols = head_cols(h)
        both[0, 1, :, cols] = dq_t[:, cols].T.astype(BF16)
    both[0, 0] = out[0]

    @pl.when(step == pl.num_programs(0) - 1)
    def _():
        dp[:, :HD] = apk[...].astype(BF16)
        dp[:, HD:] = apv[...].astype(BF16)


def whole(shape):
    return pl.BlockSpec(shape, lambda i, *_: (0,) * len(shape))


def stepped(shape):
    return pl.BlockSpec((1, *shape[1:]), lambda i, *_: (i,) + (0,) * (len(shape) - 1))


def call(body, name, scalars, steps, args, outs, scratch):
    spec = lambda shape, by_step: stepped(shape) if by_step else whole(shape)
    return pl.pallas_call(
        body,
        grid_spec=pltpu.PrefetchScalarGridSpec(
            num_scalar_prefetch=len(scalars),
            grid=(steps,),
            in_specs=[spec(a.shape, by_step) for a, by_step in args],
            out_specs=[spec(shape, by_step) for shape, _, by_step in outs],
            scratch_shapes=[pltpu.VMEM(shape, dtype) for shape, dtype in scratch],
        ),
        out_shape=[jax.ShapeDtypeStruct(shape, dtype) for shape, dtype, _ in outs],
        compiler_params=pltpu.CompilerParams(vmem_limit_bytes=60 * 1024 * 1024),
        name=name,
    )(*scalars, *[a for a, _ in args])


def prefix_forward(lengths, qg, prefix):
    n = len(qg)
    tall, rows = (n, HD, ROWS), (n, 8, ROWS)
    return call(
        prefix_kernel, "prefix_forward", [lengths], n,
        [(a, False) for a in (*qg, prefix)],
        [(tall, BF16, True), (tall, BF16, True), ((n, PREFIX, ROWS), BF16, True), (tall, F32, True),
         (rows, F32, True), ((HD, PREFIX), BF16, False)],
        [((HD, PREFIX), BF16), ((PREFIX, ROWS), F32)],
    )


def branch(parents, lengths, qt, gt, prefix_out, stats, kv):
    n = qt.shape[0]
    tall, rows, keys = (n, HD, ROWS), (n, 8, ROWS), DEPTH * BLOCK
    return call(
        branch_kernel, "branch", [parents, lengths], n,
        [(qt, True), (gt, True), (prefix_out, True), (stats, True), (kv, False)],
        [((n, BLOCK, ROWS), BF16, True), (tall, F32, True), (tall, BF16, True), (tall, BF16, True),
         (rows, F32, True), (kv.shape, BF16, False)],
        [((HD, ROWS), BF16), ((HD, ROWS), BF16), ((keys, HD), BF16), ((keys, HD), BF16),
         ((HD, keys), BF16), ((HD, keys), BF16), ((keys, ROWS), F32), ((keys, ROWS), BF16),
         ((HD + 8, ROWS), F32), ((keys, BLOCK), F32), ((NB, BLOCK, HD), F32), ((NB, BLOCK, HD), F32)],
    )


def prefix_backward(gt, probs, glp, qlp, rows_in, dq_part, out, pkt, prefix):
    n = gt.shape[0]
    return call(
        prefix_back_kernel, "prefix_backward", [], n,
        [(a, True) for a in (gt, probs, glp, qlp, rows_in, dq_part, out)] + [(pkt, False), (prefix, False)],
        [((n, 2, BLOCK, ROWS), BF16, True), (prefix.shape, BF16, False)],
        [((PREFIX, HD), F32), ((PREFIX, HD), F32)],
    )


def head_at(d):
    return lax.rem(lax.axis_index("y") + d, HK)


def pack_kernel(sources, targets):
    for d, target in enumerate(targets):
        for part in range(2):
            width = target.shape[2]
            source = sources[part % len(sources)]
            first = 0 if len(sources) > 1 else part * HK * width
            cols = pl.ds(pl.multiple_of(first + head_at(d) * width, 128), width)
            target[part] = source[:, cols]


def pack(*sources):
    rows, columns = sources[0].shape
    width = columns // (HK if len(sources) > 1 else 2 * HK)
    tile, n = min(rows, TILE), len(sources)
    return pl.pallas_call(
        lambda *refs: pack_kernel(refs[:n], refs[n:]),
        grid=(rows // tile,),
        in_specs=[pl.BlockSpec((tile, columns), lambda i: (i, 0))] * n,
        out_specs=[pl.BlockSpec((2, tile, width), lambda i: (0, i, 0))] * HK,
        out_shape=[jax.ShapeDtypeStruct((2, rows, width), BF16)] * HK,
        name="pack",
    )(*sources)


def unpack_kernel(sources, targets):
    for d, source in enumerate(sources):
        for part in range(2):
            width = source.shape[2]
            target = targets[part % len(targets)]
            first = 0 if len(targets) > 1 else part * HK * width
            cols = pl.ds(pl.multiple_of(first + head_at(d) * width, 128), width)
            target[:, cols] = source[part]


def unpack(sources, count):
    _, rows, width = sources[0].shape
    tile, n = min(rows, TILE), len(sources)
    columns = 2 * HK * width // count
    return pl.pallas_call(
        lambda *refs: unpack_kernel(refs[:n], refs[n:]),
        grid=(rows // tile,),
        in_specs=[pl.BlockSpec((2, tile, width), lambda i: (0, i, 0))] * n,
        out_specs=[pl.BlockSpec((tile, columns), lambda i: (i, 0))] * count,
        out_shape=[jax.ShapeDtypeStruct((rows, columns), BF16)] * count,
        name="unpack",
    )(*sources)


def shift(x, axis, by):
    n = lax.axis_size(axis)
    return lax.ppermute(x, axis, [(i, (i + by) % n) for i in range(n)])


def spread(x, axes):
    n = lax.axis_size(axes)
    return lax.all_to_all(jnp.broadcast_to(x, (n, *x.shape)), axes, split_axis=0, concat_axis=0, tiled=True)


def gather_terms(x, axes):
    n = lax.axis_size(axes)
    x = x.reshape(n, x.shape[0] // n, x.shape[1])
    return jnp.sum(lax.all_to_all(x, axes, split_axis=0, concat_axis=0, tiled=True).astype(F32), axis=0).astype(BF16)


def per_device(query, d_out, branch_kv, prefix_kv, parents, lengths):
    ny, nz = lax.axis_size("y"), lax.axis_size("z")

    def exchange(parts):
        return [parts[0]] + [shift(parts[d], "y", d) for d in range(1, ny)]

    def back(parts):
        return [parts[0]] + [shift(parts[d], "y", -d) for d in range(1, ny)]

    kv = exchange(pack(branch_kv[0]))
    ring, smp = ("x", "core", "y"), ("x", "core")
    half_rows = prefix_kv.shape[0] // 2
    value_holder = lax.axis_index("x") >= 2
    low, high = prefix_kv[:half_rows], prefix_kv[half_rows:]
    one = lax.ppermute(jnp.where(value_holder, low, high), ring, half_moves(0))
    two = lax.ppermute(jnp.where(value_holder, high, low), ring, half_moves(1))
    odd = lax.axis_index("core") == 1
    mine = jnp.concatenate([jnp.where(odd, one, two), jnp.where(odd, two, one)], axis=1)
    kv = lax.all_gather(jnp.stack(kv), "z", axis=0, tiled=True)
    qg = exchange(pack(query[0], d_out[0]))
    prefix = spread(spread(mine, "z").reshape(-1, 2 * HD), smp).reshape(PREFIX, 2 * HD)

    qt, gt, probs, prefix_out, stats, pkt = prefix_forward(lengths[0], qg, prefix)
    out, dq_part, glp, qlp, rows, dkv = branch(parents[0], lengths[0], qt, gt, prefix_out, stats, kv)
    dkv = lax.psum_scatter(dkv, "z", scatter_dimension=0, tiled=True)
    od, dp = prefix_backward(gt, probs, glp, qlp, rows, dq_part, out, pkt, prefix)

    mine = gather_terms(gather_terms(dp, smp), "z")
    key, value = mine[:, :HD], mine[:, HD:]
    returns = lambda first: [(b, a) for a, b in half_moves(first)]
    one = lax.ppermute(jnp.where(odd, key, value), ring, returns(0))
    two = lax.ppermute(jnp.where(odd, value, key), ring, returns(1))
    d_prefix = jnp.concatenate(
        [jnp.where(value_holder, one, two), jnp.where(value_holder, two, one)], axis=0)
    out, dq = unpack(back([od[d] for d in range(ny)]), 2)
    d_branch, = unpack(back([dkv[d] for d in range(ny)]), 1)
    return out[None], dq[None], d_branch[None], d_prefix


def solution(mesh):
    devices = mesh.devices.reshape(4, 2, 4, 8)
    split = Mesh(devices, ("x", "core", "y", "z"))
    smp, ctx = ("x", "core"), ("y", "z")
    return jax.shard_map(
        per_device,
        mesh=split,
        in_specs=(
            P(smp, ctx, None), P(smp, ctx, None), P(smp, ctx, None),
            P(ctx, smp), P(smp, None), P(smp, None),
        ),
        out_specs=(P(smp, ctx, None), P(smp, ctx, None), P(smp, ctx, None), P(ctx, smp)),
        check_vma=False,
    )
```

```python
import jax
import jax.numpy as jnp
from jax import lax
from jax.experimental import pallas as pl
from jax.experimental.pallas import tpu as pltpu
from jax.sharding import Mesh, PartitionSpec as P

HK = 4
HD = 128
GROUP = 8
BLOCK = 128
NB = 32
DEPTH = 8
PREFIX = 1024
NEAR = PREFIX + BLOCK
ROWS = GROUP * BLOCK
CHUNK = 256
TILE = 64
SCALE = HD ** -0.5
SCALE_LOG2E = SCALE * 1.4426950408889634
MASKED = -1e30
F32 = jnp.float32
BF16 = jnp.bfloat16


def dot(a, b):
    return lax.dot_general(a, b, (((1,), (0,)), ((), ())), preferred_element_type=F32)


def dot_t(a, b):
    return lax.dot_general(a, b, (((1,), (1,)), ((), ())), preferred_element_type=F32)


def my_blocks(step):
    ny, nz = lax.axis_size("y"), lax.axis_size("z")
    return lax.rem(lax.axis_index("y") - step + ny, ny) * nz + lax.axis_index("z")


def place_of(block):
    ny, nz = lax.axis_size("y"), lax.axis_size("z")
    return lax.rem(block, nz) * ny + lax.rem(lax.axis_index("y") - block // nz + ny, ny)


def half_moves(first):
    moves = []
    for feature in range(2 * HK):
        half = first if feature >= HK else 1 - first
        for holder in range(HK):
            moves.append((feature * HK + holder, (holder * 2 + half) * HK + feature % HK))
    return moves


def fold(a):
    return a.reshape(a.shape[0] // 8, 8, a.shape[1])


def head_cols(h):
    return slice(h * BLOCK, (h + 1) * BLOCK)


def live_rows(lengths, step):
    return lax.broadcasted_iota(jnp.int32, (HD, BLOCK), 1) < lengths[my_blocks(step)]


NEAR_CHUNKS = [slice(c, min(c + CHUNK, NEAR)) for c in range(0, NEAR, CHUNK)]


def near_kernel(
    lengths, q0, q1, q2, q3, prefix, own,
    qt, probs, out_t, stats, keys, keys_t, values, values_t, scores,
):
    step = pl.program_id(0)

    @pl.when(step == 0)
    def _():
        keys[:PREFIX, :] = prefix[:, :HD]
        values[:PREFIX, :] = prefix[:, HD:]
        keys_t[:, :PREFIX] = prefix[:, :HD].T
        values_t[:, :PREFIX] = prefix[:, HD:].T

    keys[PREFIX:, :] = own[0, 0]
    values[PREFIX:, :] = own[0, 1]
    values_t[:, PREFIX:] = own[0, 1].T

    for d, part in enumerate((q0, q1, q2, q3)):
        @pl.when(step == d)
        def _(part=part):
            for h in range(GROUP):
                cols = head_cols(h)
                qt[0, :, cols] = part[0, :, cols].T

    key_row = lax.broadcasted_iota(jnp.int32, (BLOCK, BLOCK), 0)
    query_row = lax.broadcasted_iota(jnp.int32, (BLOCK, BLOCK), 1)
    seen = (key_row < lengths[my_blocks(step)]) & (key_row <= query_row)
    bias = jnp.where(seen, 0.0, MASKED)
    top = jnp.full((8, ROWS), MASKED, F32)
    for rows in NEAR_CHUNKS:
        s = dot(keys[rows, :], qt[0])
        if rows.start >= PREFIX:
            s = s + jnp.concatenate([bias] * GROUP, axis=1)
        scores[rows, :] = s
        top = jnp.maximum(top, jnp.max(fold(s), axis=0))
    top = jnp.max(top, axis=0, keepdims=True)
    peak = top * SCALE_LOG2E
    total = jnp.zeros((8, ROWS), F32)
    acc = jnp.zeros((HD, ROWS), F32)
    for rows in NEAR_CHUNKS:
        e = jnp.exp2(scores[rows, :] * SCALE_LOG2E - peak)
        total = total + jnp.sum(fold(e), axis=0)
        low = e.astype(BF16)
        probs[0, rows, :] = low
        acc = acc + dot(values_t[:, rows], low)
    out_t[0] = acc
    stats[0, 0:1, :] = top
    stats[0, 1:2, :] = jnp.sum(total, axis=0, keepdims=True)


def branch_kernel(
    parents, lengths, qt, near_out, stats, g0, g1, g2, g3, kv,
    gt, out, dq_part, rows_out, dkv,
    qlt, glt, sk, sv, skt, svt, scores, probs, acc, bias, abk, abv, touched,
):
    step = pl.program_id(0)
    block = my_blocks(step)

    @pl.when(step == 0)
    def _():
        for n in range(NB):
            touched[n] = 0

    row_live = live_rows(lengths, step)
    for d, part in enumerate((g0, g1, g2, g3)):
        @pl.when(step == d)
        def _(part=part):
            for h in range(GROUP):
                cols = head_cols(h)
                gt[0, :, cols] = jnp.where(row_live, part[0, :, cols].astype(F32).T, 0.0).astype(BF16)

    slots, used = [], []
    current = parents[block]
    for k in range(DEPTH):
        in_use = current >= 0
        slot = jnp.where(in_use, current, block)
        slots.append(slot)
        used.append(in_use)
        current = jnp.where(in_use, parents[slot], -1)
    key_row = lax.broadcasted_iota(jnp.int32, (BLOCK, BLOCK), 0)
    pairs = DEPTH // 2
    acc[0:8, :] = jnp.broadcast_to(stats[0, 0:1, :], (8, ROWS))
    for j in range(pairs):
        @pl.when(used[2 * j])
        def _(j=j):
            for k in (2 * j, 2 * j + 1):
                rows = head_cols(k)
                at = place_of(slots[k])
                key = kv[at, 0]
                value = kv[at, 1]
                sk[rows, :] = key
                sv[rows, :] = value
                skt[:, rows] = key.T
                svt[:, rows] = value.T
                seen = key_row < jnp.where(used[k], lengths[slots[k]], 0)
                bias[rows, :] = jnp.where(seen, 0.0, MASKED)
            rows = slice(j * CHUNK, (j + 1) * CHUNK)
            s = dot(sk[rows, :], qt[0])
            s = s + jnp.concatenate([bias[rows, :]] * GROUP, axis=1)
            scores[rows, :] = s
            acc[0:8, :] = jnp.maximum(acc[0:8, :], jnp.max(fold(s), axis=0))
    peak = jnp.max(acc[0:8, :], axis=0, keepdims=True) * SCALE_LOG2E

    acc[...] = jnp.zeros_like(acc)
    for j in range(pairs):
        @pl.when(used[2 * j])
        def _(j=j):
            rows = slice(j * CHUNK, (j + 1) * CHUNK)
            e = jnp.exp2(scores[rows, :] * SCALE_LOG2E - peak)
            acc[HD:HD + 8, :] += jnp.sum(fold(e), axis=0)
            low = e.astype(BF16)
            probs[rows, :] = low
            acc[0:HD, :] += dot(svt[:, rows], low)

    alpha = jnp.exp2(stats[0, 0:1, :] * SCALE_LOG2E - peak)
    total = alpha * stats[0, 1:2, :] + jnp.sum(acc[HD:HD + 8, :], axis=0, keepdims=True)
    inverse = 1.0 / total
    near_inverse = alpha * inverse
    out_t = (acc[0:HD, :] * inverse + near_out[0] * near_inverse).astype(BF16)
    grad_t = gt[0].astype(F32)
    delta = jnp.sum(grad_t * out_t.astype(F32), axis=0, keepdims=True)
    glt[...] = (grad_t * inverse).astype(BF16)
    qlt[...] = (qt[0].astype(F32) * (inverse * SCALE)).astype(BF16)
    rows_out[0, 0:1, :] = delta
    rows_out[0, 1:2, :] = near_inverse
    out[0] = out_t

    acc[0:HD, :] = jnp.zeros((HD, ROWS), F32)
    for j in range(pairs):
        @pl.when(used[2 * j])
        def _(j=j):
            rows = slice(j * CHUNK, (j + 1) * CHUNK)
            low = probs[rows, :]
            ds = (low.astype(F32) * (dot(sv[rows, :], gt[0]) - delta)).astype(BF16)
            dv = dot_t(low, glt[...])
            dk = dot_t(ds, qlt[...])
            for k in range(2):
                at = place_of(slots[2 * j + k])
                had = touched[at] > 0
                abv[at] = jnp.where(had, abv[at], 0.0) + dv[k * BLOCK:(k + 1) * BLOCK]
                abk[at] = jnp.where(had, abk[at], 0.0) + dk[k * BLOCK:(k + 1) * BLOCK]
                touched[at] = 1
            acc[0:HD, :] += dot(skt[:, rows], ds)
    dq_part[0] = acc[0:HD, :] * (inverse * SCALE)

    @pl.when(step == pl.num_programs(0) - 1)
    def _():
        for n in range(NB):
            @pl.when(touched[n] > 0)
            def _(n=n):
                dkv[n, 0] = abk[n].astype(BF16)
                dkv[n, 1] = abv[n].astype(BF16)

            @pl.when(touched[n] == 0)
            def _(n=n):
                dkv[n] = jnp.zeros((2, BLOCK, HD), BF16)


def near_back_kernel(
    lengths, qt, gt, probs, rows_in, dq_part, out, prefix, own,
    both, d_own, dp, keys_t, values, apk, apv, qln, gln,
):
    step = pl.program_id(0)

    @pl.when(step == 0)
    def _():
        keys_t[:, :PREFIX] = prefix[:, :HD].T
        values[:PREFIX, :] = prefix[:, HD:]
        apk[...] = jnp.zeros_like(apk)
        apv[...] = jnp.zeros_like(apv)

    keys_t[:, PREFIX:] = own[0, 0].T
    values[PREFIX:, :] = own[0, 1]
    delta = rows_in[0, 0:1, :]
    inverse = rows_in[0, 1:2, :]
    gln[...] = (gt[0].astype(F32) * inverse).astype(BF16)
    qln[...] = (qt[0].astype(F32) * (inverse * SCALE)).astype(BF16)
    acc = jnp.zeros((HD, ROWS), F32)
    for rows in NEAR_CHUNKS:
        low = probs[0, rows, :]
        ds = (low.astype(F32) * (dot(values[rows, :], gt[0]) - delta)).astype(BF16)
        dv = dot_t(low, gln[...])
        dk = dot_t(ds, qln[...])
        if rows.start >= PREFIX:
            d_own[0, 0] = dk
            d_own[0, 1] = dv
        else:
            apk[rows, :] += dk
            apv[rows, :] += dv
        acc = acc + dot(keys_t[:, rows], ds)
    dq_t = acc * (inverse * SCALE) + dq_part[0]
    row_live = live_rows(lengths, step)
    for h in range(GROUP):
        cols = head_cols(h)
        both[0, 0, :, cols] = jnp.where(row_live, out[0, :, cols].astype(F32), 0.0).T.astype(BF16)
        both[0, 1, :, cols] = dq_t[:, cols].T.astype(BF16)

    @pl.when(step == pl.num_programs(0) - 1)
    def _():
        dp[:, :HD] = apk[...].astype(BF16)
        dp[:, HD:] = apv[...].astype(BF16)


def whole(shape):
    return pl.BlockSpec(shape, lambda i, *_: (0,) * len(shape))


def stepped(shape):
    return pl.BlockSpec((1, *shape[1:]), lambda i, *_: (i,) + (0,) * (len(shape) - 1))


def call(body, name, scalars, steps, args, outs, scratch, more=[]):
    spec = lambda shape, by_step: stepped(shape) if by_step else whole(shape)
    return pl.pallas_call(
        body,
        grid_spec=pltpu.PrefetchScalarGridSpec(
            num_scalar_prefetch=len(scalars),
            grid=(steps,),
            in_specs=[spec(a.shape, by_step) for a, by_step in args],
            out_specs=[spec(shape, by_step) for shape, _, by_step in outs],
            scratch_shapes=[pltpu.VMEM(shape, dtype) for shape, dtype in scratch] + more,
        ),
        out_shape=[jax.ShapeDtypeStruct(shape, dtype) for shape, dtype, _ in outs],
        compiler_params=pltpu.CompilerParams(vmem_limit_bytes=60 * 1024 * 1024),
        name=name,
    )(*scalars, *[a for a, _ in args])


def near_forward(lengths, q, prefix, own):
    n = len(q)
    tall, rows = (n, HD, ROWS), (n, 8, ROWS)
    return call(
        near_kernel, "near_forward", [lengths], n,
        [(a, False) for a in (*q, prefix)] + [(own, True)],
        [(tall, BF16, True), ((n, NEAR, ROWS), BF16, True), (tall, F32, True), (rows, F32, True)],
        [((NEAR, HD), BF16), ((HD, NEAR), BF16), ((NEAR, HD), BF16), ((HD, NEAR), BF16), ((NEAR, ROWS), F32)],
    )


def branch(parents, lengths, qt, near_out, stats, g, kv):
    n = qt.shape[0]
    tall, rows, keys = (n, HD, ROWS), (n, 8, ROWS), DEPTH * BLOCK
    return call(
        branch_kernel, "branch", [parents, lengths], n,
        [(qt, True), (near_out, True), (stats, True)] + [(a, False) for a in (*g, kv)],
        [(tall, BF16, True), (tall, BF16, True), (tall, F32, True), (rows, F32, True), (kv.shape, BF16, False)],
        [((HD, ROWS), BF16), ((HD, ROWS), BF16), ((keys, HD), BF16), ((keys, HD), BF16),
         ((HD, keys), BF16), ((HD, keys), BF16), ((keys, ROWS), F32), ((keys, ROWS), BF16),
         ((HD + 8, ROWS), F32), ((keys, BLOCK), F32), ((NB, BLOCK, HD), F32), ((NB, BLOCK, HD), F32)],
        [pltpu.SMEM((NB,), jnp.int32)],
    )


def near_backward(lengths, qt, gt, probs, rows_in, dq_part, out, prefix, own):
    n = gt.shape[0]
    return call(
        near_back_kernel, "near_backward", [lengths], n,
        [(a, True) for a in (qt, gt, probs, rows_in, dq_part, out)] + [(prefix, False), (own, True)],
        [((n, 2, BLOCK, ROWS), BF16, True), (own.shape, F32, True), (prefix.shape, BF16, False)],
        [((HD, NEAR), BF16), ((NEAR, HD), BF16), ((PREFIX, HD), F32), ((PREFIX, HD), F32),
         ((HD, ROWS), BF16), ((HD, ROWS), BF16)],
    )


def head_at(d):
    return lax.rem(lax.axis_index("y") + d, HK)


def pack_kernel(source, *targets):
    for d, target in enumerate(targets):
        parts, _, width = target.shape
        for part in range(parts):
            cols = pl.ds(pl.multiple_of((part * HK + head_at(d)) * width, 128), width)
            target[part] = source[:, cols]


def pack(source, parts):
    rows, columns = source.shape
    width = columns // (HK * parts)
    return pl.pallas_call(
        pack_kernel,
        grid=(rows // TILE,),
        in_specs=[pl.BlockSpec((TILE, columns), lambda i: (i, 0))],
        out_specs=[pl.BlockSpec((parts, TILE, width), lambda i: (0, i, 0))] * HK,
        out_shape=[jax.ShapeDtypeStruct((parts, rows, width), BF16)] * HK,
        name="pack",
    )(source)


def unpack_kernel(sources, targets):
    for d, source in enumerate(sources):
        for part in range(2):
            width = source.shape[2]
            target = targets[part % len(targets)]
            first = 0 if len(targets) > 1 else part * HK * width
            cols = pl.ds(pl.multiple_of(first + head_at(d) * width, 128), width)
            target[:, cols] = source[part]


def unpack(sources, count):
    _, rows, width = sources[0].shape
    tile, n = min(rows, TILE), len(sources)
    columns = 2 * HK * width // count
    return pl.pallas_call(
        lambda *refs: unpack_kernel(refs[:n], refs[n:]),
        grid=(rows // tile,),
        in_specs=[pl.BlockSpec((2, tile, width), lambda i: (0, i, 0))] * n,
        out_specs=[pl.BlockSpec((tile, columns), lambda i: (i, 0))] * count,
        out_shape=[jax.ShapeDtypeStruct((rows, columns), BF16)] * count,
        name="unpack",
    )(*sources)


def shift(x, axis, by):
    n = lax.axis_size(axis)
    return lax.ppermute(x, axis, [(i, (i + by) % n) for i in range(n)])


def spread(x, axes):
    n = lax.axis_size(axes)
    return lax.all_to_all(jnp.broadcast_to(x, (n, *x.shape)), axes, split_axis=0, concat_axis=0, tiled=True)


def gather_terms(x, axes):
    n = lax.axis_size(axes)
    x = x.reshape(n, x.shape[0] // n, x.shape[1])
    return jnp.sum(lax.all_to_all(x, axes, split_axis=0, concat_axis=0, tiled=True).astype(F32), axis=0).astype(BF16)


def per_device(query, d_out, branch_kv, prefix_kv, parents, lengths):
    ny, nz = lax.axis_size("y"), lax.axis_size("z")

    def exchange(parts):
        return [parts[0]] + [shift(parts[d], "y", d) for d in range(1, ny)]

    def back(parts):
        return [parts[0]] + [shift(parts[d], "y", -d) for d in range(1, ny)]

    kv = exchange(pack(branch_kv[0], 2))
    q = pack(query[0], 1)
    kv, q, d_out = lax.optimization_barrier((kv, q, d_out))
    q = exchange(q)
    ring, smp = ("x", "core", "y"), ("x", "core")
    half_rows = prefix_kv.shape[0] // 2
    value_holder = lax.axis_index("x") >= 2
    low, high = prefix_kv[:half_rows], prefix_kv[half_rows:]
    one = lax.ppermute(jnp.where(value_holder, low, high), ring, half_moves(0))
    two = lax.ppermute(jnp.where(value_holder, high, low), ring, half_moves(1))
    odd = lax.axis_index("core") == 1
    mine = jnp.concatenate([jnp.where(odd, one, two), jnp.where(odd, two, one)], axis=1)
    own = jnp.stack(kv)
    kv = lax.all_gather(own, "z", axis=0, tiled=True)
    g = exchange(pack(d_out[0], 1))
    prefix = spread(mine, "z").reshape(-1, 2 * HD)
    prefix, q = lax.optimization_barrier((prefix, q))
    prefix = spread(prefix, smp).reshape(PREFIX, 2 * HD)

    qt, probs, near_out, stats = near_forward(lengths[0], q, prefix, own)
    gt, out, dq_part, rows, dkv = branch(parents[0], lengths[0], qt, near_out, stats, g, kv)
    dkv = lax.psum_scatter(dkv, "z", scatter_dimension=0, tiled=True)
    od, d_own, dp = near_backward(lengths[0], qt, gt, probs, rows, dq_part, out, prefix, own)

    mine = gather_terms(gather_terms(dp, smp), "z")
    key, value = mine[:, :HD], mine[:, HD:]
    returns = lambda first: [(b, a) for a, b in half_moves(first)]
    one = lax.ppermute(jnp.where(odd, key, value), ring, returns(0))
    two = lax.ppermute(jnp.where(odd, value, key), ring, returns(1))
    d_prefix = jnp.concatenate(
        [jnp.where(value_holder, one, two), jnp.where(value_holder, two, one)], axis=0)
    out, dq = unpack(back([od[d] for d in range(ny)]), 2)
    dkv = (dkv.astype(F32) + d_own).astype(BF16)
    d_branch, = unpack(back([dkv[d] for d in range(ny)]), 1)
    return out[None], dq[None], d_branch[None], d_prefix


def solution(mesh):
    devices = mesh.devices.reshape(4, 2, 4, 8)
    split = Mesh(devices, ("x", "core", "y", "z"))
    smp, ctx = ("x", "core"), ("y", "z")
    return jax.shard_map(
        per_device,
        mesh=split,
        in_specs=(
            P(smp, ctx, None), P(smp, ctx, None), P(smp, ctx, None),
            P(ctx, smp), P(smp, None), P(smp, None),
        ),
        out_specs=(P(smp, ctx, None), P(smp, ctx, None), P(smp, ctx, None), P(ctx, smp)),
        check_vma=False,
    )
```

```python
import jax
import jax.numpy as jnp
from jax import lax
from jax.experimental import pallas as pl
from jax.experimental.pallas import tpu as pltpu
from jax.sharding import Mesh, PartitionSpec as P

HK = 4
HD = 128
GROUP = 8
BLOCK = 128
NB = 32
DEPTH = 8
PREFIX = 1024
NEAR = PREFIX + BLOCK
ROWS = GROUP * BLOCK
CHUNK = 256
TILE = 64
SCALE = HD ** -0.5
SCALE_LOG2E = SCALE * 1.4426950408889634
MASKED = -1e30
F32 = jnp.float32
BF16 = jnp.bfloat16


def dot(a, b):
    return lax.dot_general(a, b, (((1,), (0,)), ((), ())), preferred_element_type=F32)


def dot_t(a, b):
    return lax.dot_general(a, b, (((1,), (1,)), ((), ())), preferred_element_type=F32)


def my_blocks(step):
    ny, nz = lax.axis_size("y"), lax.axis_size("z")
    return lax.rem(lax.axis_index("y") - step + ny, ny) * nz + lax.axis_index("z")


def place_of(block):
    ny, nz = lax.axis_size("y"), lax.axis_size("z")
    return lax.rem(block, nz) * ny + lax.rem(lax.axis_index("y") - block // nz + ny, ny)


def half_moves(first):
    moves = []
    for feature in range(2 * HK):
        half = first if feature >= HK else 1 - first
        for holder in range(HK):
            moves.append((feature * HK + holder, (holder * 2 + half) * HK + feature % HK))
    return moves


def fold(a):
    return a.reshape(a.shape[0] // 8, 8, a.shape[1])


def head_cols(h):
    return slice(h * BLOCK, (h + 1) * BLOCK)


def live_rows(lengths, step):
    return lax.broadcasted_iota(jnp.int32, (HD, BLOCK), 1) < lengths[my_blocks(step)]


NEAR_CHUNKS = [slice(c, min(c + CHUNK, NEAR)) for c in range(0, NEAR, CHUNK)]


def near_kernel(
    lengths, q0, q1, q2, q3, prefix, own,
    qt, probs, out_t, stats, keys, keys_t, values, values_t, scores,
):
    step = pl.program_id(0)

    @pl.when(step == 0)
    def _():
        keys[:PREFIX, :] = prefix[:, :HD]
        values[:PREFIX, :] = prefix[:, HD:]
        keys_t[:, :PREFIX] = prefix[:, :HD].T
        values_t[:, :PREFIX] = prefix[:, HD:].T

    keys[PREFIX:, :] = own[0, 0]
    values[PREFIX:, :] = own[0, 1]
    values_t[:, PREFIX:] = own[0, 1].T

    for d, part in enumerate((q0, q1, q2, q3)):
        @pl.when(step == d)
        def _(part=part):
            for h in range(GROUP):
                cols = head_cols(h)
                qt[0, :, cols] = part[0, :, cols].T

    key_row = lax.broadcasted_iota(jnp.int32, (BLOCK, BLOCK), 0)
    query_row = lax.broadcasted_iota(jnp.int32, (BLOCK, BLOCK), 1)
    seen = (key_row < lengths[my_blocks(step)]) & (key_row <= query_row)
    bias = jnp.where(seen, 0.0, MASKED)
    top = jnp.full((8, ROWS), MASKED, F32)
    for rows in NEAR_CHUNKS:
        s = dot(keys[rows, :], qt[0])
        if rows.start >= PREFIX:
            s = s + jnp.concatenate([bias] * GROUP, axis=1)
        scores[rows, :] = s
        top = jnp.maximum(top, jnp.max(fold(s), axis=0))
    top = jnp.max(top, axis=0, keepdims=True)
    peak = top * SCALE_LOG2E
    total = jnp.zeros((8, ROWS), F32)
    acc = jnp.zeros((HD, ROWS), F32)
    for rows in NEAR_CHUNKS:
        e = jnp.exp2(scores[rows, :] * SCALE_LOG2E - peak)
        total = total + jnp.sum(fold(e), axis=0)
        low = e.astype(BF16)
        probs[0, rows, :] = low
        acc = acc + dot(values_t[:, rows], low)
    out_t[0] = acc
    stats[0, 0:1, :] = top
    stats[0, 1:2, :] = jnp.sum(total, axis=0, keepdims=True)


def branch_kernel(
    parents, lengths, qt, near_out, stats, g0, g1, g2, g3, kv,
    gt, out, dq_part, rows_out, dkv,
    qlt, glt, sk, sv, skt, svt, scores, probs, acc, bias, abk, abv, touched,
):
    step = pl.program_id(0)
    block = my_blocks(step)

    @pl.when(step == 0)
    def _():
        for n in range(NB):
            touched[n] = 0

    row_live = live_rows(lengths, step)
    for d, part in enumerate((g0, g1, g2, g3)):
        @pl.when(step == d)
        def _(part=part):
            for h in range(GROUP):
                cols = head_cols(h)
                gt[0, :, cols] = jnp.where(row_live, part[0, :, cols].astype(F32).T, 0.0).astype(BF16)

    slots, used = [], []
    current = parents[block]
    for k in range(DEPTH):
        in_use = current >= 0
        slot = jnp.where(in_use, current, block)
        slots.append(slot)
        used.append(in_use)
        current = jnp.where(in_use, parents[slot], -1)
    key_row = lax.broadcasted_iota(jnp.int32, (BLOCK, BLOCK), 0)
    pairs = DEPTH // 2
    acc[0:8, :] = jnp.broadcast_to(stats[0, 0:1, :], (8, ROWS))
    for j in range(pairs):
        @pl.when(used[2 * j])
        def _(j=j):
            for k in (2 * j, 2 * j + 1):
                rows = head_cols(k)
                at = place_of(slots[k])
                key = kv[at, 0]
                value = kv[at, 1]
                sk[rows, :] = key
                sv[rows, :] = value
                skt[:, rows] = key.T
                svt[:, rows] = value.T
                seen = key_row < jnp.where(used[k], lengths[slots[k]], 0)
                bias[rows, :] = jnp.where(seen, 0.0, MASKED)
            rows = slice(j * CHUNK, (j + 1) * CHUNK)
            s = dot(sk[rows, :], qt[0])
            s = s + jnp.concatenate([bias[rows, :]] * GROUP, axis=1)
            scores[rows, :] = s
            acc[0:8, :] = jnp.maximum(acc[0:8, :], jnp.max(fold(s), axis=0))
    peak = jnp.max(acc[0:8, :], axis=0, keepdims=True) * SCALE_LOG2E

    acc[...] = jnp.zeros_like(acc)
    for j in range(pairs):
        @pl.when(used[2 * j])
        def _(j=j):
            rows = slice(j * CHUNK, (j + 1) * CHUNK)
            e = jnp.exp2(scores[rows, :] * SCALE_LOG2E - peak)
            acc[HD:HD + 8, :] += jnp.sum(fold(e), axis=0)
            low = e.astype(BF16)
            probs[rows, :] = low
            acc[0:HD, :] += dot(svt[:, rows], low)

    alpha = jnp.exp2(stats[0, 0:1, :] * SCALE_LOG2E - peak)
    total = alpha * stats[0, 1:2, :] + jnp.sum(acc[HD:HD + 8, :], axis=0, keepdims=True)
    inverse = 1.0 / total
    near_inverse = alpha * inverse
    out_t = (acc[0:HD, :] * inverse + near_out[0] * near_inverse).astype(BF16)
    grad_t = gt[0].astype(F32)
    delta = jnp.sum(grad_t * out_t.astype(F32), axis=0, keepdims=True)
    glt[...] = (grad_t * inverse).astype(BF16)
    qlt[...] = (qt[0].astype(F32) * (inverse * SCALE)).astype(BF16)
    rows_out[0, 0:1, :] = delta
    rows_out[0, 1:2, :] = near_inverse
    out[0] = out_t

    acc[0:HD, :] = jnp.zeros((HD, ROWS), F32)
    for j in range(pairs):
        @pl.when(used[2 * j])
        def _(j=j):
            rows = slice(j * CHUNK, (j + 1) * CHUNK)
            low = probs[rows, :]
            ds = (low.astype(F32) * (dot(sv[rows, :], gt[0]) - delta)).astype(BF16)
            dv = dot_t(low, glt[...])
            dk = dot_t(ds, qlt[...])
            for k in range(2):
                at = place_of(slots[2 * j + k])
                had = touched[at] > 0
                abv[at] = jnp.where(had, abv[at], 0.0) + dv[k * BLOCK:(k + 1) * BLOCK]
                abk[at] = jnp.where(had, abk[at], 0.0) + dk[k * BLOCK:(k + 1) * BLOCK]
                touched[at] = 1
            acc[0:HD, :] += dot(skt[:, rows], ds)
    dq_part[0] = acc[0:HD, :] * (inverse * SCALE)

    @pl.when(step == pl.num_programs(0) - 1)
    def _():
        for n in range(NB):
            @pl.when(touched[n] > 0)
            def _(n=n):
                dkv[n, 0] = abk[n].astype(BF16)
                dkv[n, 1] = abv[n].astype(BF16)

            @pl.when(touched[n] == 0)
            def _(n=n):
                dkv[n] = jnp.zeros((2, BLOCK, HD), BF16)


def near_back_kernel(
    lengths, qt, gt, probs, rows_in, dq_part, out, prefix, own,
    od0, od1, od2, od3, d_own, dp, keys_t, values, apk, apv, qln, gln,
):
    step = pl.program_id(0)

    @pl.when(step == 0)
    def _():
        keys_t[:, :PREFIX] = prefix[:, :HD].T
        values[:PREFIX, :] = prefix[:, HD:]
        apk[...] = jnp.zeros_like(apk)
        apv[...] = jnp.zeros_like(apv)

    keys_t[:, PREFIX:] = own[0, 0].T
    values[PREFIX:, :] = own[0, 1]
    delta = rows_in[0, 0:1, :]
    inverse = rows_in[0, 1:2, :]
    gln[...] = (gt[0].astype(F32) * inverse).astype(BF16)
    qln[...] = (qt[0].astype(F32) * (inverse * SCALE)).astype(BF16)
    acc = jnp.zeros((HD, ROWS), F32)
    for rows in NEAR_CHUNKS:
        low = probs[0, rows, :]
        ds = (low.astype(F32) * (dot(values[rows, :], gt[0]) - delta)).astype(BF16)
        dv = dot_t(low, gln[...])
        dk = dot_t(ds, qln[...])
        if rows.start >= PREFIX:
            d_own[0, 0] = dk
            d_own[0, 1] = dv
        else:
            apk[rows, :] += dk
            apv[rows, :] += dv
        acc = acc + dot(keys_t[:, rows], ds)
    dq_t = acc * (inverse * SCALE) + dq_part[0]
    row_live = live_rows(lengths, step)
    for d, both in enumerate((od0, od1, od2, od3)):
        @pl.when(step == d)
        def _(both=both):
            for h in range(GROUP):
                cols = head_cols(h)
                both[0, :, cols] = jnp.where(row_live, out[0, :, cols].astype(F32), 0.0).T.astype(BF16)
                both[1, :, cols] = dq_t[:, cols].T.astype(BF16)

    @pl.when(step == pl.num_programs(0) - 1)
    def _():
        dp[:, :HD] = apk[...].astype(BF16)
        dp[:, HD:] = apv[...].astype(BF16)


def whole(shape):
    return pl.BlockSpec(shape, lambda i, *_: (0,) * len(shape))


def stepped(shape):
    return pl.BlockSpec((1, *shape[1:]), lambda i, *_: (i,) + (0,) * (len(shape) - 1))


def call(body, name, scalars, steps, args, outs, scratch, more=[]):
    spec = lambda shape, by_step: stepped(shape) if by_step else whole(shape)
    return pl.pallas_call(
        body,
        grid_spec=pltpu.PrefetchScalarGridSpec(
            num_scalar_prefetch=len(scalars),
            grid=(steps,),
            in_specs=[spec(a.shape, by_step) for a, by_step in args],
            out_specs=[spec(shape, by_step) for shape, _, by_step in outs],
            scratch_shapes=[pltpu.VMEM(shape, dtype) for shape, dtype in scratch] + more,
        ),
        out_shape=[jax.ShapeDtypeStruct(shape, dtype) for shape, dtype, _ in outs],
        compiler_params=pltpu.CompilerParams(vmem_limit_bytes=60 * 1024 * 1024),
        name=name,
    )(*scalars, *[a for a, _ in args])


def near_forward(lengths, q, prefix, own):
    n = len(q)
    tall, rows = (n, HD, ROWS), (n, 8, ROWS)
    return call(
        near_kernel, "near_forward", [lengths], n,
        [(a, False) for a in (*q, prefix)] + [(own, True)],
        [(tall, BF16, True), ((n, NEAR, ROWS), BF16, True), (tall, F32, True), (rows, F32, True)],
        [((NEAR, HD), BF16), ((HD, NEAR), BF16), ((NEAR, HD), BF16), ((HD, NEAR), BF16), ((NEAR, ROWS), F32)],
    )


def branch(parents, lengths, qt, near_out, stats, g, kv):
    n = qt.shape[0]
    tall, rows, keys = (n, HD, ROWS), (n, 8, ROWS), DEPTH * BLOCK
    return call(
        branch_kernel, "branch", [parents, lengths], n,
        [(qt, True), (near_out, True), (stats, True)] + [(a, False) for a in (*g, kv)],
        [(tall, BF16, True), (tall, BF16, True), (tall, F32, True), (rows, F32, True), (kv.shape, BF16, False)],
        [((HD, ROWS), BF16), ((HD, ROWS), BF16), ((keys, HD), BF16), ((keys, HD), BF16),
         ((HD, keys), BF16), ((HD, keys), BF16), ((keys, ROWS), F32), ((keys, ROWS), BF16),
         ((HD + 8, ROWS), F32), ((keys, BLOCK), F32), ((NB, BLOCK, HD), F32), ((NB, BLOCK, HD), F32)],
        [pltpu.SMEM((NB,), jnp.int32)],
    )


def near_backward(lengths, qt, gt, probs, rows_in, dq_part, out, prefix, own):
    n = gt.shape[0]
    return call(
        near_back_kernel, "near_backward", [lengths], n,
        [(a, True) for a in (qt, gt, probs, rows_in, dq_part, out)] + [(prefix, False), (own, True)],
        [((2, BLOCK, ROWS), BF16, False)] * n + [(own.shape, F32, True), (prefix.shape, BF16, False)],
        [((HD, NEAR), BF16), ((NEAR, HD), BF16), ((PREFIX, HD), F32), ((PREFIX, HD), F32),
         ((HD, ROWS), BF16), ((HD, ROWS), BF16)],
    )


def head_at(d):
    return lax.rem(lax.axis_index("y") + d, HK)


def pack_kernel(source, *targets):
    for d, target in enumerate(targets):
        parts, _, width = target.shape
        for part in range(parts):
            cols = pl.ds(pl.multiple_of((part * HK + head_at(d)) * width, 128), width)
            target[part] = source[:, cols]


def pack(source, parts):
    rows, columns = source.shape
    width = columns // (HK * parts)
    return pl.pallas_call(
        pack_kernel,
        grid=(rows // TILE,),
        in_specs=[pl.BlockSpec((TILE, columns), lambda i: (i, 0))],
        out_specs=[pl.BlockSpec((parts, TILE, width), lambda i: (0, i, 0))] * HK,
        out_shape=[jax.ShapeDtypeStruct((parts, rows, width), BF16)] * HK,
        name="pack",
    )(source)


def unpack_kernel(sources, targets):
    for d, source in enumerate(sources):
        for part in range(2):
            width = source.shape[2]
            target = targets[part % len(targets)]
            first = 0 if len(targets) > 1 else part * HK * width
            cols = pl.ds(pl.multiple_of(first + head_at(d) * width, 128), width)
            target[:, cols] = source[part]


def unpack(sources, count):
    _, rows, width = sources[0].shape
    tile, n = min(rows, TILE), len(sources)
    columns = 2 * HK * width // count
    return pl.pallas_call(
        lambda *refs: unpack_kernel(refs[:n], refs[n:]),
        grid=(rows // tile,),
        in_specs=[pl.BlockSpec((2, tile, width), lambda i: (0, i, 0))] * n,
        out_specs=[pl.BlockSpec((tile, columns), lambda i: (i, 0))] * count,
        out_shape=[jax.ShapeDtypeStruct((rows, columns), BF16)] * count,
        name="unpack",
    )(*sources)


def shift(x, axis, by):
    n = lax.axis_size(axis)
    return lax.ppermute(x, axis, [(i, (i + by) % n) for i in range(n)])


def spread(x, axes):
    n = lax.axis_size(axes)
    return lax.all_to_all(jnp.broadcast_to(x, (n, *x.shape)), axes, split_axis=0, concat_axis=0, tiled=True)


def gather_terms(x, axes):
    n = lax.axis_size(axes)
    x = x.reshape(n, x.shape[0] // n, x.shape[1])
    return jnp.sum(lax.all_to_all(x, axes, split_axis=0, concat_axis=0, tiled=True).astype(F32), axis=0).astype(BF16)


def per_device(query, d_out, branch_kv, prefix_kv, parents, lengths):
    ny, nz = lax.axis_size("y"), lax.axis_size("z")

    def exchange(parts):
        return [parts[0]] + [shift(parts[d], "y", d) for d in range(1, ny)]

    def back(parts):
        return [parts[0]] + [shift(parts[d], "y", -d) for d in range(1, ny)]

    kv = exchange(pack(branch_kv[0], 2))
    q = pack(query[0], 1)
    kv, q, d_out = lax.optimization_barrier((kv, q, d_out))
    q = exchange(q)
    ring, smp = ("x", "core", "y"), ("x", "core")
    half_rows = prefix_kv.shape[0] // 2
    value_holder = lax.axis_index("x") >= 2
    low, high = prefix_kv[:half_rows], prefix_kv[half_rows:]
    one = lax.ppermute(jnp.where(value_holder, low, high), ring, half_moves(0))
    two = lax.ppermute(jnp.where(value_holder, high, low), ring, half_moves(1))
    odd = lax.axis_index("core") == 1
    mine = jnp.concatenate([jnp.where(odd, one, two), jnp.where(odd, two, one)], axis=1)
    own = jnp.stack(kv)
    kv = lax.all_gather(own, "z", axis=0, tiled=True)
    g = exchange(pack(d_out[0], 1))
    prefix = spread(mine, "z").reshape(-1, 2 * HD)
    prefix, q = lax.optimization_barrier((prefix, q))
    prefix = spread(prefix, smp).reshape(PREFIX, 2 * HD)

    qt, probs, near_out, stats = near_forward(lengths[0], q, prefix, own)
    gt, out, dq_part, rows, dkv = branch(parents[0], lengths[0], qt, near_out, stats, g, kv)
    dkv = lax.psum_scatter(dkv, "z", scatter_dimension=0, tiled=True)
    *od, d_own, dp = near_backward(lengths[0], qt, gt, probs, rows, dq_part, out, prefix, own)

    mine = gather_terms(gather_terms(dp, smp), "z")
    key, value = mine[:, :HD], mine[:, HD:]
    returns = lambda first: [(b, a) for a, b in half_moves(first)]
    one = lax.ppermute(jnp.where(odd, key, value), ring, returns(0))
    two = lax.ppermute(jnp.where(odd, value, key), ring, returns(1))
    d_prefix = jnp.concatenate(
        [jnp.where(value_holder, one, two), jnp.where(value_holder, two, one)], axis=0)
    out, dq = unpack(back(od), 2)
    dkv = (dkv.astype(F32) + d_own).astype(BF16)
    d_branch, = unpack(back([dkv[d] for d in range(ny)]), 1)
    return out[None], dq[None], d_branch[None], d_prefix


def solution(mesh):
    devices = mesh.devices.reshape(4, 2, 4, 8)
    split = Mesh(devices, ("x", "core", "y", "z"))
    smp, ctx = ("x", "core"), ("y", "z")
    return jax.shard_map(
        per_device,
        mesh=split,
        in_specs=(
            P(smp, ctx, None), P(smp, ctx, None), P(smp, ctx, None),
            P(ctx, smp), P(smp, None), P(smp, None),
        ),
        out_specs=(P(smp, ctx, None), P(smp, ctx, None), P(smp, ctx, None), P(ctx, smp)),
        check_vma=False,
    )
```

```python
import jax
import jax.numpy as jnp
from jax import lax
from jax.experimental import pallas as pl
from jax.experimental.pallas import tpu as pltpu
from jax.sharding import Mesh, PartitionSpec as P

HK = 4
HD = 128
GROUP = 8
BLOCK = 128
NB = 32
DEPTH = 8
PREFIX = 1024
NEAR = PREFIX + BLOCK
ROWS = GROUP * BLOCK
CHUNK = 256
TILE = 64
SCALE = HD ** -0.5
SCALE_LOG2E = SCALE * 1.4426950408889634
MASKED = -1e30
F32 = jnp.float32
BF16 = jnp.bfloat16


def dot(a, b):
    return lax.dot_general(a, b, (((1,), (0,)), ((), ())), preferred_element_type=F32)


def dot_t(a, b):
    return lax.dot_general(a, b, (((1,), (1,)), ((), ())), preferred_element_type=F32)


def my_blocks(step):
    ny, nz = lax.axis_size("y"), lax.axis_size("z")
    return lax.rem(lax.axis_index("y") - step + ny, ny) * nz + lax.axis_index("z")


def place_of(block):
    ny, nz = lax.axis_size("y"), lax.axis_size("z")
    return lax.rem(block, nz) * ny + lax.rem(lax.axis_index("y") - block // nz + ny, ny)


def half_moves(first):
    moves = []
    for feature in range(2 * HK):
        half = first if feature >= HK else 1 - first
        for holder in range(HK):
            moves.append((feature * HK + holder, (holder * 2 + half) * HK + feature % HK))
    return moves


def fold(a):
    return a.reshape(a.shape[0] // 8, 8, a.shape[1])


def head_cols(h):
    return slice(h * BLOCK, (h + 1) * BLOCK)


def live_rows(lengths, step):
    return lax.broadcasted_iota(jnp.int32, (HD, BLOCK), 1) < lengths[my_blocks(step)]


NEAR_CHUNKS = [slice(c, min(c + CHUNK, NEAR)) for c in range(0, NEAR, CHUNK)]


def near_kernel(
    lengths, q0, q1, q2, q3, prefix, own,
    qt, probs, out_t, stats, keys, keys_t, values, values_t, scores,
):
    step = pl.program_id(0)

    @pl.when(step == 0)
    def _():
        keys[:PREFIX, :] = prefix[:, :HD]
        values[:PREFIX, :] = prefix[:, HD:]
        keys_t[:, :PREFIX] = prefix[:, :HD].T
        values_t[:, :PREFIX] = prefix[:, HD:].T

    keys[PREFIX:, :] = own[0, 0]
    values[PREFIX:, :] = own[0, 1]
    values_t[:, PREFIX:] = own[0, 1].T

    for d, part in enumerate((q0, q1, q2, q3)):
        @pl.when(step == d)
        def _(part=part):
            for h in range(GROUP):
                cols = head_cols(h)
                qt[0, :, cols] = part[0, :, cols].T

    key_row = lax.broadcasted_iota(jnp.int32, (BLOCK, BLOCK), 0)
    query_row = lax.broadcasted_iota(jnp.int32, (BLOCK, BLOCK), 1)
    seen = (key_row < lengths[my_blocks(step)]) & (key_row <= query_row)
    bias = jnp.where(seen, 0.0, MASKED)
    top = jnp.full((8, ROWS), MASKED, F32)
    for rows in NEAR_CHUNKS:
        s = dot(keys[rows, :], qt[0])
        if rows.start >= PREFIX:
            s = s + jnp.concatenate([bias] * GROUP, axis=1)
        scores[rows, :] = s
        top = jnp.maximum(top, jnp.max(fold(s), axis=0))
    top = jnp.max(top, axis=0, keepdims=True)
    peak = top * SCALE_LOG2E
    total = jnp.zeros((8, ROWS), F32)
    acc = jnp.zeros((HD, ROWS), F32)
    for rows in NEAR_CHUNKS:
        e = jnp.exp2(scores[rows, :] * SCALE_LOG2E - peak)
        total = total + jnp.sum(fold(e), axis=0)
        low = e.astype(BF16)
        probs[0, rows, :] = low
        acc = acc + dot(values_t[:, rows], low)
    out_t[0] = acc
    stats[0, 0:1, :] = top
    stats[0, 1:2, :] = jnp.sum(total, axis=0, keepdims=True)


def branch_kernel(
    parents, lengths, qt, near_out, stats, g0, g1, g2, g3, kv,
    gt, out, dq_part, rows_out, dkv,
    qlt, glt, sk, sv, skt, svt, scores, probs, acc, bias, abk, abv, touched,
):
    step = pl.program_id(0)
    block = my_blocks(step)

    @pl.when(step == 0)
    def _():
        for n in range(NB):
            touched[n] = 0

    row_live = live_rows(lengths, step)
    for d, part in enumerate((g0, g1, g2, g3)):
        @pl.when(step == d)
        def _(part=part):
            for h in range(GROUP):
                cols = head_cols(h)
                gt[0, :, cols] = jnp.where(row_live, part[0, :, cols].astype(F32).T, 0.0).astype(BF16)

    slots, used = [], []
    current = parents[block]
    for k in range(DEPTH):
        in_use = current >= 0
        slot = jnp.where(in_use, current, block)
        slots.append(slot)
        used.append(in_use)
        current = jnp.where(in_use, parents[slot], -1)
    key_row = lax.broadcasted_iota(jnp.int32, (BLOCK, BLOCK), 0)
    pairs = DEPTH // 2
    acc[0:8, :] = jnp.broadcast_to(stats[0, 0:1, :], (8, ROWS))
    for j in range(pairs):
        @pl.when(used[2 * j])
        def _(j=j):
            for k in (2 * j, 2 * j + 1):
                rows = head_cols(k)
                at = place_of(slots[k])
                key = kv[at, 0]
                value = kv[at, 1]
                sk[rows, :] = key
                sv[rows, :] = value
                skt[:, rows] = key.T
                svt[:, rows] = value.T
                seen = key_row < jnp.where(used[k], lengths[slots[k]], 0)
                bias[rows, :] = jnp.where(seen, 0.0, MASKED)
            rows = slice(j * CHUNK, (j + 1) * CHUNK)
            s = dot(sk[rows, :], qt[0])
            s = s + jnp.concatenate([bias[rows, :]] * GROUP, axis=1)
            scores[rows, :] = s
            acc[0:8, :] = jnp.maximum(acc[0:8, :], jnp.max(fold(s), axis=0))
    peak = jnp.max(acc[0:8, :], axis=0, keepdims=True) * SCALE_LOG2E

    acc[...] = jnp.zeros_like(acc)
    for j in range(pairs):
        @pl.when(used[2 * j])
        def _(j=j):
            rows = slice(j * CHUNK, (j + 1) * CHUNK)
            e = jnp.exp2(scores[rows, :] * SCALE_LOG2E - peak)
            acc[HD:HD + 8, :] += jnp.sum(fold(e), axis=0)
            low = e.astype(BF16)
            probs[rows, :] = low
            acc[0:HD, :] += dot(svt[:, rows], low)

    alpha = jnp.exp2(stats[0, 0:1, :] * SCALE_LOG2E - peak)
    total = alpha * stats[0, 1:2, :] + jnp.sum(acc[HD:HD + 8, :], axis=0, keepdims=True)
    inverse = 1.0 / total
    near_inverse = alpha * inverse
    out_t = (acc[0:HD, :] * inverse + near_out[0] * near_inverse).astype(BF16)
    grad_t = gt[0].astype(F32)
    delta = jnp.sum(grad_t * out_t.astype(F32), axis=0, keepdims=True)
    glt[...] = (grad_t * inverse).astype(BF16)
    qlt[...] = (qt[0].astype(F32) * (inverse * SCALE)).astype(BF16)
    rows_out[0, 0:1, :] = delta
    rows_out[0, 1:2, :] = near_inverse
    out[0] = out_t

    acc[0:HD, :] = jnp.zeros((HD, ROWS), F32)
    for j in range(pairs):
        @pl.when(used[2 * j])
        def _(j=j):
            rows = slice(j * CHUNK, (j + 1) * CHUNK)
            low = probs[rows, :]
            ds = (low.astype(F32) * (dot(sv[rows, :], gt[0]) - delta)).astype(BF16)
            dv = dot_t(low, glt[...])
            dk = dot_t(ds, qlt[...])
            for k in range(2):
                at = place_of(slots[2 * j + k])
                had = touched[at] > 0
                abv[at] = jnp.where(had, abv[at], 0.0) + dv[k * BLOCK:(k + 1) * BLOCK]
                abk[at] = jnp.where(had, abk[at], 0.0) + dk[k * BLOCK:(k + 1) * BLOCK]
                touched[at] = 1
            acc[0:HD, :] += dot(skt[:, rows], ds)
    dq_part[0] = acc[0:HD, :] * (inverse * SCALE)

    @pl.when(step == pl.num_programs(0) - 1)
    def _():
        for n in range(NB):
            @pl.when(touched[n] > 0)
            def _(n=n):
                dkv[n, 0] = abk[n].astype(BF16)
                dkv[n, 1] = abv[n].astype(BF16)

            @pl.when(touched[n] == 0)
            def _(n=n):
                dkv[n] = jnp.zeros((2, BLOCK, HD), BF16)


def near_back_kernel(
    lengths, qt, gt, probs, rows_in, dq_part, out, prefix, own,
    both, d_own, dp, keys_t, values, apk, apv, qln, gln,
):
    step = pl.program_id(0)

    @pl.when(step == 0)
    def _():
        keys_t[:, :PREFIX] = prefix[:, :HD].T
        values[:PREFIX, :] = prefix[:, HD:]
        apk[...] = jnp.zeros_like(apk)
        apv[...] = jnp.zeros_like(apv)

    keys_t[:, PREFIX:] = own[0, 0].T
    values[PREFIX:, :] = own[0, 1]
    delta = rows_in[0, 0:1, :]
    inverse = rows_in[0, 1:2, :]
    gln[...] = (gt[0].astype(F32) * inverse).astype(BF16)
    qln[...] = (qt[0].astype(F32) * (inverse * SCALE)).astype(BF16)
    acc = jnp.zeros((HD, ROWS), F32)
    for rows in NEAR_CHUNKS:
        low = probs[0, rows, :]
        ds = (low.astype(F32) * (dot(values[rows, :], gt[0]) - delta)).astype(BF16)
        dv = dot_t(low, gln[...])
        dk = dot_t(ds, qln[...])
        if rows.start >= PREFIX:
            d_own[0, 0] = dk
            d_own[0, 1] = dv
        else:
            apk[rows, :] += dk
            apv[rows, :] += dv
        acc = acc + dot(keys_t[:, rows], ds)
    dq_t = acc * (inverse * SCALE) + dq_part[0]
    row_live = live_rows(lengths, step)
    for h in range(GROUP):
        cols = head_cols(h)
        both[0, 0, :, cols] = jnp.where(row_live, out[0, :, cols].astype(F32), 0.0).T.astype(BF16)
        both[0, 1, :, cols] = dq_t[:, cols].T.astype(BF16)

    @pl.when(step == pl.num_programs(0) - 1)
    def _():
        dp[:, :HD] = apk[...].astype(BF16)
        dp[:, HD:] = apv[...].astype(BF16)


def whole(shape):
    return pl.BlockSpec(shape, lambda i, *_: (0,) * len(shape))


def stepped(shape):
    return pl.BlockSpec((1, *shape[1:]), lambda i, *_: (i,) + (0,) * (len(shape) - 1))


def call(body, name, scalars, steps, args, outs, scratch, more=[]):
    spec = lambda shape, by_step: stepped(shape) if by_step else whole(shape)
    return pl.pallas_call(
        body,
        grid_spec=pltpu.PrefetchScalarGridSpec(
            num_scalar_prefetch=len(scalars),
            grid=(steps,),
            in_specs=[spec(a.shape, by_step) for a, by_step in args],
            out_specs=[spec(shape, by_step) for shape, _, by_step in outs],
            scratch_shapes=[pltpu.VMEM(shape, dtype) for shape, dtype in scratch] + more,
        ),
        out_shape=[jax.ShapeDtypeStruct(shape, dtype) for shape, dtype, _ in outs],
        compiler_params=pltpu.CompilerParams(vmem_limit_bytes=(60 if name == "branch" else 40) * 1024 * 1024),
        name=name,
    )(*scalars, *[a for a, _ in args])


def near_forward(lengths, q, prefix, own):
    n = len(q)
    tall, rows = (n, HD, ROWS), (n, 8, ROWS)
    return call(
        near_kernel, "near_forward", [lengths], n,
        [(a, False) for a in (*q, prefix)] + [(own, True)],
        [(tall, BF16, True), ((n, NEAR, ROWS), BF16, True), (tall, F32, True), (rows, F32, True)],
        [((NEAR, HD), BF16), ((HD, NEAR), BF16), ((NEAR, HD), BF16), ((HD, NEAR), BF16), ((NEAR, ROWS), F32)],
    )


def branch(parents, lengths, qt, near_out, stats, g, kv):
    n = qt.shape[0]
    tall, rows, keys = (n, HD, ROWS), (n, 8, ROWS), DEPTH * BLOCK
    return call(
        branch_kernel, "branch", [parents, lengths], n,
        [(qt, True), (near_out, True), (stats, True)] + [(a, False) for a in (*g, kv)],
        [(tall, BF16, True), (tall, BF16, True), (tall, F32, True), (rows, F32, True), (kv.shape, BF16, False)],
        [((HD, ROWS), BF16), ((HD, ROWS), BF16), ((keys, HD), BF16), ((keys, HD), BF16),
         ((HD, keys), BF16), ((HD, keys), BF16), ((keys, ROWS), F32), ((keys, ROWS), BF16),
         ((HD + 8, ROWS), F32), ((keys, BLOCK), F32), ((NB, BLOCK, HD), F32), ((NB, BLOCK, HD), F32)],
        [pltpu.SMEM((NB,), jnp.int32)],
    )


def near_backward(lengths, qt, gt, probs, rows_in, dq_part, out, prefix, own):
    n = gt.shape[0]
    return call(
        near_back_kernel, "near_backward", [lengths], n,
        [(a, True) for a in (qt, gt, probs, rows_in, dq_part, out)] + [(prefix, False), (own, True)],
        [((n, 2, BLOCK, ROWS), BF16, True), (own.shape, F32, True), (prefix.shape, BF16, False)],
        [((HD, NEAR), BF16), ((NEAR, HD), BF16), ((PREFIX, HD), F32), ((PREFIX, HD), F32),
         ((HD, ROWS), BF16), ((HD, ROWS), BF16)],
    )


def head_at(d):
    return lax.rem(lax.axis_index("y") + d, HK)


def pack_kernel(source, *targets):
    for d, target in enumerate(targets):
        parts, _, width = target.shape
        for part in range(parts):
            cols = pl.ds(pl.multiple_of((part * HK + head_at(d)) * width, 128), width)
            target[part] = source[:, cols]


def pack(source, parts):
    rows, columns = source.shape
    width = columns // (HK * parts)
    return pl.pallas_call(
        pack_kernel,
        grid=(rows // TILE,),
        in_specs=[pl.BlockSpec((TILE, columns), lambda i: (i, 0))],
        out_specs=[pl.BlockSpec((parts, TILE, width), lambda i: (0, i, 0))] * HK,
        out_shape=[jax.ShapeDtypeStruct((parts, rows, width), BF16)] * HK,
        name="pack",
    )(source)


def unpack_kernel(sources, targets):
    for d, source in enumerate(sources):
        for part in range(2):
            width = source.shape[2]
            target = targets[part % len(targets)]
            first = 0 if len(targets) > 1 else part * HK * width
            cols = pl.ds(pl.multiple_of(first + head_at(d) * width, 128), width)
            target[:, cols] = source[part]


def unpack(sources, count):
    _, rows, width = sources[0].shape
    tile, n = min(rows, TILE), len(sources)
    columns = 2 * HK * width // count
    return pl.pallas_call(
        lambda *refs: unpack_kernel(refs[:n], refs[n:]),
        grid=(rows // tile,),
        in_specs=[pl.BlockSpec((2, tile, width), lambda i: (0, i, 0))] * n,
        out_specs=[pl.BlockSpec((tile, columns), lambda i: (i, 0))] * count,
        out_shape=[jax.ShapeDtypeStruct((rows, columns), BF16)] * count,
        name="unpack",
    )(*sources)


def shift(x, axis, by):
    n = lax.axis_size(axis)
    return lax.ppermute(x, axis, [(i, (i + by) % n) for i in range(n)])


def spread(x, axes):
    n = lax.axis_size(axes)
    return lax.all_to_all(jnp.broadcast_to(x, (n, *x.shape)), axes, split_axis=0, concat_axis=0, tiled=True)


def gather_terms(x, axes):
    n = lax.axis_size(axes)
    x = x.reshape(n, x.shape[0] // n, x.shape[1])
    return jnp.sum(lax.all_to_all(x, axes, split_axis=0, concat_axis=0, tiled=True).astype(F32), axis=0).astype(BF16)


def per_device(query, d_out, branch_kv, prefix_kv, parents, lengths):
    ny, nz = lax.axis_size("y"), lax.axis_size("z")

    def exchange(parts):
        return [parts[0]] + [shift(parts[d], "y", d) for d in range(1, ny)]

    def back(parts):
        return [parts[0]] + [shift(parts[d], "y", -d) for d in range(1, ny)]

    kv = exchange(pack(branch_kv[0], 2))
    q = pack(query[0], 1)
    kv, q, d_out = lax.optimization_barrier((kv, q, d_out))
    q = exchange(q)
    ring, smp = ("x", "core", "y"), ("x", "core")
    half_rows = prefix_kv.shape[0] // 2
    value_holder = lax.axis_index("x") >= 2
    low, high = prefix_kv[:half_rows], prefix_kv[half_rows:]
    one = lax.ppermute(jnp.where(value_holder, low, high), ring, half_moves(0))
    two = lax.ppermute(jnp.where(value_holder, high, low), ring, half_moves(1))
    odd = lax.axis_index("core") == 1
    mine = jnp.concatenate([jnp.where(odd, one, two), jnp.where(odd, two, one)], axis=1)
    own = jnp.stack(kv)
    kv = lax.all_gather(own, "z", axis=0, tiled=True)
    g = exchange(pack(d_out[0], 1))
    prefix = spread(mine, "z").reshape(-1, 2 * HD)
    prefix, q = lax.optimization_barrier((prefix, q))
    prefix = spread(prefix, smp).reshape(PREFIX, 2 * HD)

    qt, probs, near_out, stats = near_forward(lengths[0], q, prefix, own)
    gt, out, dq_part, rows, dkv = branch(parents[0], lengths[0], qt, near_out, stats, g, kv)
    dkv = lax.psum_scatter(dkv, "z", scatter_dimension=0, tiled=True)
    od, d_own, dp = near_backward(lengths[0], qt, gt, probs, rows, dq_part, out, prefix, own)

    mine = gather_terms(gather_terms(dp, smp), "z")
    key, value = mine[:, :HD], mine[:, HD:]
    returns = lambda first: [(b, a) for a, b in half_moves(first)]
    one = lax.ppermute(jnp.where(odd, key, value), ring, returns(0))
    two = lax.ppermute(jnp.where(odd, value, key), ring, returns(1))
    d_prefix = jnp.concatenate(
        [jnp.where(value_holder, one, two), jnp.where(value_holder, two, one)], axis=0)
    out, dq = unpack(back([od[d] for d in range(ny)]), 2)
    dkv = (dkv.astype(F32) + d_own).astype(BF16)
    d_branch, = unpack(back([dkv[d] for d in range(ny)]), 1)
    return out[None], dq[None], d_branch[None], d_prefix


def solution(mesh):
    devices = mesh.devices.reshape(4, 2, 4, 8)
    split = Mesh(devices, ("x", "core", "y", "z"))
    smp, ctx = ("x", "core"), ("y", "z")
    return jax.shard_map(
        per_device,
        mesh=split,
        in_specs=(
            P(smp, ctx, None), P(smp, ctx, None), P(smp, ctx, None),
            P(ctx, smp), P(smp, None), P(smp, None),
        ),
        out_specs=(P(smp, ctx, None), P(smp, ctx, None), P(smp, ctx, None), P(ctx, smp)),
        check_vma=False,
    )
```
